32 devices in a mesh: req: 8 (over y, x, core), mlp: 4 (over z).
Axes of the slice: x: 2, y: 2, z: 4, core: 2. Of those that a mesh axis runs over, the one named last changes fastest.
Arguments:
- tokens: bfloat16 [1024, 2048], P(('req', 'mlp')), may hold values from -6 to 6
- cached_states: float32 [64, 8, 256, 512], P('req', 'mlp'), may hold values from -12 to 12
- prompt_lengths: int32 [64], P('req'), may hold values from 1 to 4096, as said below
- accepted: int32 [64], P('req'), may hold values from 1 to 16, as said below
- owner_slot: int32 [64], P('req'), may hold values from 0 to 63, as said below
- w_query: bfloat16 [2048, 2048], P(None, 'mlp'), may hold values from -0.125 to 0.125
- w_key: bfloat16 [2048, 2048], P(None, 'mlp'), may hold values from -0.125 to 0.125
- w_value: bfloat16 [2048, 4096], P(None, 'mlp'), may hold values from -0.125 to 0.125
- w_gate_ret: bfloat16 [2048, 4096], P(None, 'mlp'), may hold values from -0.125 to 0.125
- w_out: bfloat16 [4096, 2048], P('mlp'), may hold values from -0.09375 to 0.09375
- w_gate: bfloat16 [2048, 4096], P('req', 'mlp'), may hold values from -0.125 to 0.125
- w_up: bfloat16 [2048, 4096], P('req', 'mlp'), may hold values from -0.125 to 0.125
- w_down: bfloat16 [4096, 2048], P('mlp', 'req'), may hold values from -0.09375 to 0.09375
Outputs:
- mixed: bfloat16 [1024, 2048], P(('req', 'mlp'))
- new_states: float32 [64, 8, 256, 512], P('req', 'mlp')
The draws below stay inside these ranges and needn't reach their ends.
Inputs may be any that keep to these rules, and one draw needn't show every extreme that they name: `prompt_lengths`: request r belongs to tenant k = (4 r) // 64, so the four tenants hold consecutive ranges of 16 requests; its prompt length is drawn evenly from 1 to 4^(k + 3). `accepted`: number of leading drafts of request r that are kept, drawn evenly for each request. A permutation of the requests; for request r on req block i = r // 8, owner_slot[r] = j * 8 + i + c with owner block j and 0 <= c < 1, and each pair (j, c) occurs exactly once within a block.
All inputs are finite; a program needn't handle non-finite values.
Results may differ from the reference program's by a relative error of at most 0.017.
Values may be sent and summed in bfloat16 or wider, within the bound.
A program may use at most 128 MiB of HBM per device.

```python
import math
import jax
import jax.numpy as jnp
from jax import lax

D = 2048
HEADS = 8
DK = 256
DV = 512
FF = 4096
DRAFT = 16
PER_PEER = 1
REQ_DEV = 8
NREQ = 64
TOKENS = 1024
N_REQ = 8


def draw_owner_slot(key, part):
    sub_keys = jax.random.split(jax.random.fold_in(key, 7), N_REQ)
    shuffled = jax.vmap(lambda one_key: jax.random.permutation(one_key, REQ_DEV))(sub_keys)
    sources = jnp.arange(N_REQ, dtype=jnp.int32)[:, None]
    slots = shuffled // PER_PEER * REQ_DEV + sources * PER_PEER + shuffled % PER_PEER
    return slots.reshape(-1).astype(jnp.int32)


def draw_prompt_lengths(key, part):
    request_ids = jnp.arange(NREQ, dtype=jnp.int32)
    tenant = 4 * request_ids // NREQ
    limit = jnp.left_shift(jnp.ones_like(request_ids), 2 * tenant + 6)
    drawn = jax.random.randint(jax.random.fold_in(key, 11), (NREQ,), 0, 4096, dtype=jnp.int32) % limit + 1
    leading = request_ids == tenant * (NREQ // 4)
    drawn = jnp.where(leading, limit, drawn)
    drawn = jnp.where(request_ids == 1, jnp.ones_like(drawn), drawn)
    return drawn.astype(jnp.int32)


def draw_accepted(key, part):
    request_ids = jnp.arange(NREQ, dtype=jnp.int32)
    drawn = jax.random.randint(jax.random.fold_in(key, 13), (NREQ,), 1, DRAFT + 1, dtype=jnp.int32)
    drawn = jnp.where(request_ids == 0, jnp.full_like(drawn, DRAFT), drawn)
    drawn = jnp.where(request_ids == 2, jnp.ones_like(drawn), drawn)
    return drawn.astype(jnp.int32)


def shard_levels(key, shape, shards, smallest, high):
    factor_of, own = 1.0, jax.random.fold_in(key, 6)
    for position, parts in shards:
        draws = jnp.exp(jax.random.uniform(jax.random.fold_in(own, position), (parts,), jnp.float32, smallest / len(shards), high / len(shards)))
        factor_of = factor_of * jnp.repeat(draws, shape[position] // parts).reshape([-1 if axis == position else 1 for axis in range(len(shape))])
    return factor_of


def gaussian(own_key, extent, spread, most, pieces=(), held_as=jnp.bfloat16):
    values = jax.random.normal(own_key, extent, jnp.float32) * spread
    if len(pieces) > 0:
        values = shard_levels(own_key, extent, pieces, -0.22, 0.18) * values
    return jnp.clip(values, min=-most, max=most).astype(held_as)


def setup_inputs(seed: int = 0) -> dict:
    splits = jax.random.split(jax.random.key(seed), 14)
    tokens = gaussian(splits[0], (TOKENS, D), 1.0, 6.0, ((0, 32),))
    cached_states = gaussian(splits[1], (NREQ, HEADS, DK, DV), 2.0, 12.0, ((0, 8), (1, 4)), jnp.float32)
    prompt_lengths = draw_prompt_lengths(jax.random.fold_in(splits[13], 71), 0)
    accepted = draw_accepted(jax.random.fold_in(splits[13], 71), 0)
    owner_slot = draw_owner_slot(jax.random.fold_in(splits[13], 71), 0)
    w_query = gaussian(splits[5], (D, HEADS * DK), D ** -0.5, 0.125, ((1, 4),))
    w_key = gaussian(splits[6], (D, HEADS * DK), D ** -0.5, 0.125, ((1, 4),))
    w_value = gaussian(splits[7], (D, HEADS * DV), D ** -0.5, 0.125, ((1, 4),))
    w_gate_ret = gaussian(splits[8], (D, HEADS * DV), D ** -0.5, 0.125, ((1, 4),))
    w_out = gaussian(splits[9], (HEADS * DV, D), (HEADS * DV) ** -0.5, 0.09375, ((0, 4),))
    w_gate = gaussian(splits[10], (D, FF), D ** -0.5, 0.125, ((0, 8), (1, 4)))
    w_up = gaussian(splits[11], (D, FF), D ** -0.5, 0.125, ((0, 8), (1, 4)))
    w_down = gaussian(splits[12], (FF, D), FF ** -0.5, 0.09375, ((0, 4), (1, 8)))
    return dict(tokens=tokens, cached_states=cached_states, prompt_lengths=prompt_lengths, accepted=accepted, owner_slot=owner_slot, w_query=w_query, w_key=w_key, w_value=w_value, w_gate_ret=w_gate_ret, w_out=w_out, w_gate=w_gate, w_up=w_up, w_down=w_down)


epsilon = 1e-05

def layer_norm(inputs):
    average = lax.optimization_barrier(jnp.mean(inputs, axis=-1, keepdims=True))
    centred = inputs - average
    variance = lax.optimization_barrier(jnp.mean(centred * centred, axis=-1, keepdims=True))
    return centred * lax.rsqrt(variance + epsilon)

def decays(head_count, first_head):
    head_index = jnp.arange(head_count, dtype=jnp.float32) + first_head
    return 1.0 - jnp.exp2(-5.0 - head_index)

def rotate(inputs, positions):
    half_width = inputs.shape[-1] // 2
    frequencies = jnp.exp(-math.log(10000.0) * jnp.arange(half_width, dtype=jnp.float32) / half_width)
    angles = positions[:, :, None] * frequencies[None, None, :]
    cosine_part = jnp.cos(angles)[:, :, None, :]
    sine_part = jnp.sin(angles)[:, :, None, :]
    front_half = inputs[..., :half_width]
    back_half = inputs[..., half_width:]
    return jnp.concatenate([front_half * cosine_part - back_half * sine_part, front_half * sine_part + back_half * cosine_part], axis=-1)

def retention(queries, key_rows, values, states, accepted, gammas):
    draft_count = queries.shape[1]
    draft_pos = jnp.arange(draft_count, dtype=jnp.float32)
    distance = draft_pos[:, None] - draft_pos[None, :]
    decay_mask = jnp.where(distance[None] >= 0, jnp.power(gammas[:, None, None], jnp.maximum(distance, 0.0)[None]), 0.0)
    scores = jnp.einsum('rthd,rshd->rhts', queries.astype(jnp.float32), key_rows.astype(jnp.float32))
    weights = (scores * decay_mask[None]).astype(jnp.bfloat16)
    within = jnp.einsum('rhts,rshv->rthv', weights.astype(jnp.float32), values.astype(jnp.float32))
    carried = jnp.einsum('rthd,rhdv->rthv', queries.astype(jnp.float32), states, precision=lax.Precision.HIGHEST)
    carried = carried * jnp.power(gammas[None, None, :, None], draft_pos[None, :, None, None] + 1.0)
    outputs = within + carried
    accepted_f = accepted.astype(jnp.float32)
    exponent = accepted_f[:, None, None] - 1.0 - draft_pos[None, None, :]
    draft_weights = jnp.where(exponent >= 0, jnp.power(gammas[None, :, None], jnp.maximum(exponent, 0.0)), 0.0)
    old_part = jnp.power(gammas[None, :], accepted_f[:, None])[:, :, None, None] * states
    scaled = key_rows.astype(jnp.float32) * jnp.transpose(draft_weights, (0, 2, 1))[..., None]
    update = jnp.einsum('rshd,rshv->rhdv', scaled, values.astype(jnp.float32), precision=lax.Precision.HIGHEST)
    return (outputs, old_part + update)

def reference(tokens, cached_states, prompt_lengths, accepted, owner_slot, w_query, w_key, w_value, w_gate_ret, w_out, w_gate, w_up, w_down):
    normed = layer_norm(tokens.astype(jnp.float32)).astype(jnp.bfloat16)
    queries = jnp.dot(normed, w_query, preferred_element_type=jnp.float32).reshape(NREQ, DRAFT, HEADS, DK)
    key_rows = (jnp.dot(normed, w_key, preferred_element_type=jnp.float32) * (1.0 / math.sqrt(DK))).reshape(NREQ, DRAFT, HEADS, DK)
    values = jnp.dot(normed, w_value, preferred_element_type=jnp.float32).astype(jnp.bfloat16).reshape(NREQ, DRAFT, HEADS, DV)
    gate_ret = jnp.dot(normed, w_gate_ret, preferred_element_type=jnp.float32).reshape(NREQ, DRAFT, HEADS, DV)
    positions = (prompt_lengths[:, None] + jnp.arange(DRAFT, dtype=jnp.int32)[None, :]).astype(jnp.float32)
    rotated_q = rotate(queries, positions).astype(jnp.bfloat16)
    rotated_k = rotate(key_rows, positions).astype(jnp.bfloat16)
    gammas = decays(HEADS, 0.0)

    def one_request(item):
        result = retention(item[0][None], item[1][None], item[2][None], item[3][None], item[4][None], gammas)
        return (result[0][0], result[1][0])
    outputs, fresh = lax.map(one_request, (rotated_q, rotated_k, values, cached_states, accepted))
    joined = (layer_norm(outputs) * jax.nn.silu(gate_ret)).astype(jnp.bfloat16).reshape(NREQ * DRAFT, HEADS * DV)
    residual = tokens.astype(jnp.float32) + jnp.dot(joined, w_out, preferred_element_type=jnp.float32)
    hidden_in = layer_norm(residual).astype(jnp.bfloat16)
    gate_sum = jnp.dot(hidden_in, w_gate, preferred_element_type=jnp.float32)
    up_sum = jnp.dot(hidden_in, w_up, preferred_element_type=jnp.float32)
    hidden = (jax.nn.silu(gate_sum) * up_sum).astype(jnp.bfloat16)
    mixed = (residual + jnp.dot(hidden, w_down, preferred_element_type=jnp.float32)).astype(jnp.bfloat16)
    new_states = jnp.zeros_like(cached_states).at[owner_slot].set(fresh)
    return (mixed, new_states)
```

```python
import functools
import math

import jax
import jax.numpy as jnp
from jax import lax
from jax.experimental import pallas as pl
from jax.experimental.pallas import tpu as pltpu
from jax.sharding import PartitionSpec as P

DRAFT = 16


epsilon = 1e-05


def layer_norm(inputs):
    average = jnp.mean(inputs, axis=-1, keepdims=True)
    centred = inputs - average
    variance = jnp.mean(centred * centred, axis=-1, keepdims=True)
    return centred * lax.rsqrt(variance + epsilon)


def decays(head_count, first_head):
    head_index = jnp.arange(head_count, dtype=jnp.float32) + first_head
    return 1.0 - jnp.exp2(-5.0 - head_index)


MESH = pl.DeviceIdType.MESH
F32 = jnp.float32
BF16 = jnp.bfloat16


def mm(a, b):
    return jnp.dot(a, b, preferred_element_type=F32)


def kernel(
    n,
    m,
    order,
    old_scale,
    cosine,
    sine,
    mask,
    carry,
    fold,
    tokens,
    states,
    w_query,
    w_key,
    w_value,
    w_gate_ret,
    w_out,
    w_gate,
    w_up,
    w_down,
    mixed,
    moved,
    wq,
    wk,
    wv,
    wgr,
    wo,
    st,
    fg,
    fu,
    fd,
    tok,
    normed,
    rq,
    ksc,
    vals,
    rk_h,
    gated,
    outs,
    joined,
    part,
    part_in,
    res,
    hid,
    hs,
    part2,
    part2_in,
    send_buf,
    load_sem,
    tok_s,
    tok_r,
    part_s,
    part_r,
    hid_s,
    hid_r,
    part2_s,
    part2_r,
    w_s,
    w_r,
    st_s,
    st_r,
):
    me = lax.axis_index("req")
    mj = lax.axis_index("mlp")
    share, width = tokens.shape
    requests, heads, dk, dv = states.shape
    rows = m * share
    half = dk // 2
    per_peer = requests // n
    draft = DRAFT

    barrier = pltpu.get_barrier_semaphore()
    for k in range(1, n):
        pl.semaphore_signal(
            barrier, inc=1, device_id={"req": lax.rem(me + k, n)}, device_id_type=MESH
        )
    for k in range(1, m):
        pl.semaphore_signal(
            barrier, inc=1, device_id={"mlp": lax.rem(mj + k, m)}, device_id_type=MESH
        )

    loads = []
    for a, b in (
        (tokens, tok.at[mj]),
        (w_query, wq),
        (w_key, wk),
        (w_value, wv),
        (w_gate_ret, wgr),
        (states, st),
        (w_out, wo),
        (w_gate, fg.at[me]),
        (w_up, fu.at[me]),
        (w_down, fd.at[me]),
    ):
        copy = pltpu.make_async_copy(a, b, load_sem.at[len(loads)])
        copy.start()
        loads.append(copy)

    pl.semaphore_wait(barrier, n + m - 2)

    def mlp_copies(pick, dst, s, r):
        copies = []
        for k in range(1, m):
            peer = lax.rem(mj + k, m)
            copies.append(
                pltpu.make_async_remote_copy(
                    src_ref=pick(peer),
                    dst_ref=dst(k),
                    send_sem=s.at[k - 1],
                    recv_sem=r.at[k - 1],
                    device_id={"mlp": peer},
                    device_id_type=MESH,
                )
            )
        for copy in copies:
            copy.start()
        return copies

    tok_copies = mlp_copies(lambda peer: tokens, lambda k: tok.at[mj], tok_s, tok_r)

    cut = w_down.shape[0] // 2
    first = pl.ds(0, cut)
    second = pl.ds(cut, cut)

    def pieces(owner, own):
        if own:
            source = (w_gate, w_down.at[first], w_up, w_down.at[second])
        else:
            source = None
        there = (fg.at[owner], fd.at[owner, first], fu.at[owner], fd.at[owner, second])
        return source or there, there

    w_copies = {}

    def send_shard(owner, own, peer, slot, which=(0, 1, 2, 3)):
        source, there = pieces(owner, own)
        for i in which:
            copy = pltpu.make_async_remote_copy(
                src_ref=source[i],
                dst_ref=there[i],
                send_sem=w_s.at[slot, i],
                recv_sem=w_r.at[slot, i],
                device_id={"req": peer},
                device_id_type=MESH,
            )
            copy.start()
            w_copies[slot, i] = copy

    def arrived(slot, which=(0, 1, 2, 3)):
        for i in which:
            w_copies[slot, i].wait_recv()

    def flip(bits):
        out = me
        for bit in (1, 2, 4):
            if bits & bit:
                out = out + bit - 2 * bit * lax.rem(out // bit, 2)
        return out

    if n == 8:
        send_shard(me, True, flip(2), 0)
        send_shard(me, True, flip(4), 1)
        send_shard(me, True, flip(1), 2)
    else:
        for k in range(1, n):
            send_shard(me, True, lax.rem(me + k, n), k - 1)

    loads[0].wait()
    for copy in tok_copies:
        copy.wait_recv()
    normed[...] = layer_norm(tok[...].astype(F32).reshape(rows, width)).astype(BF16)
    cos_part, sin_part = cosine[...], sine[...]

    def turned(v):
        front, back = v[:, :half], v[:, half:]
        return jnp.concatenate(
            [front * cos_part - back * sin_part, front * sin_part + back * cos_part], axis=-1
        ).astype(BF16)

    loads[1].wait()
    loads[2].wait()
    for h in range(heads):
        cols = pl.ds(h * dk, dk)
        rq[:, cols] = turned(mm(normed[...], wq[:, cols]))
        rk = turned(mm(normed[...], wk[:, cols]) * (1.0 / math.sqrt(dk)))
        rk_h[:, cols] = rk
        ksc[:, :, cols] = (
            (rk.astype(F32) * fold[h]).astype(BF16).reshape(requests, draft, dk)
        )
    loads[3].wait()
    loads[4].wait()
    for h in range(heads):
        cols = pl.ds(h * dv, dv)
        vals[:, :, cols] = mm(normed[...], wv[:, cols]).astype(BF16).reshape(
            requests, draft, dv
        )
        g = mm(normed[...], wgr[:, cols])
        gated[:, cols] = g / (1.0 + jnp.exp(-g))
    loads[5].wait()

    @pl.loop(0, requests)
    def _(r):
        here = pl.ds(pl.multiple_of(r * draft, draft), draft)
        for h in range(heads):
            outs[here, h * dv : (h + 1) * dv] = mm(
                rq[here, h * dk : (h + 1) * dk], st[r, h].astype(BF16)
            )

    for h in range(heads):
        cols = pl.ds(h * dk, dk)
        vcols = pl.ds(h * dv, dv)
        scores = lax.dot_general(
            rq[:, cols], rk_h[:, cols], (((1,), (1,)), ((), ())), preferred_element_type=F32
        )
        weights = (scores * mask[h]).astype(BF16)
        out = mm(weights, vals[:, :, vcols].reshape(rows, dv)) + outs[:, vcols] * carry[h]
        joined[:, vcols] = (layer_norm(out) * gated[:, vcols]).astype(BF16)

    loads[6].wait()
    step = min(512, width)

    @pl.loop(0, width // step)
    def _(c):
        cols = pl.ds(pl.multiple_of(c * step, step), step)
        part[:, :, cols] = mm(joined[...], wo[:, cols]).astype(BF16).reshape(m, share, step)

    part_copies = mlp_copies(
        lambda peer: part.at[peer], lambda k: part_in.at[k - 1], part_s, part_r
    )

    if n == 8:
        arrived(0)
        send_shard(flip(2), False, flip(4), 3, (0, 1))
        arrived(1)
        send_shard(flip(4), False, flip(2), 3, (2, 3))
        send_shard(flip(2), False, flip(1), 4)
        send_shard(flip(4), False, flip(1), 5)

    st_copies = []

    def fresh(p):
        r = order[p]
        for h in range(heads):
            update = lax.dot_general(
                ksc[r, :, h * dk : (h + 1) * dk],
                vals[r, :, h * dv : (h + 1) * dv],
                (((0,), (0,)), ((), ())),
                preferred_element_type=F32,
            )
            send_buf[p, h] = (old_scale[r, h] * st[r, h] + update).astype(BF16)

    pl.loop(0, requests)(fresh)
    mine = pl.ds(me * per_peer, per_peer)
    for k in range(1, n):
        peer = lax.rem(me + k, n)
        copy = pltpu.make_async_remote_copy(
            src_ref=send_buf.at[pl.ds(peer * per_peer, per_peer)],
            dst_ref=moved.at[mine],
            send_sem=st_s.at[k - 1],
            recv_sem=st_r.at[k - 1],
            device_id={"req": peer},
            device_id_type=MESH,
        )
        copy.start()
        st_copies.append(copy)
    keep = pltpu.make_async_copy(send_buf.at[mine], moved.at[mine], load_sem.at[10])
    keep.start()

    total = part[mj].astype(F32)
    for k, copy in enumerate(part_copies):
        copy.wait_recv()
        total = total + part_in[k].astype(F32)
    residual = tok[mj].astype(F32) + total
    res[...] = residual
    hid[mj] = layer_norm(residual).astype(BF16)
    hid_copies = mlp_copies(lambda peer: hid.at[mj], lambda k: hid.at[mj], hid_s, hid_r)

    if n == 8:
        arrived(3)
        send_shard(flip(6), False, flip(1), 6)
        last = (2, 4, 5, 6)
    else:
        last = tuple(range(n - 1))
    for copy in hid_copies:
        copy.wait_recv()
    for slot in last:
        arrived(slot)
    for copy in loads[7:]:
        copy.wait()

    rows_in = fg.shape[1]
    inner = fg.shape[2]
    tile = min(256, inner)

    @pl.loop(0, inner // tile)
    def _(c):
        cols = pl.ds(pl.multiple_of(c * tile, tile), tile)
        g = jnp.zeros((rows, tile), F32)
        u = jnp.zeros((rows, tile), F32)
        for i in range(n):
            a = hid[:, :, i * rows_in : (i + 1) * rows_in].reshape(rows, rows_in)
            g = g + mm(a, fg[i, :, cols])
            u = u + mm(a, fu[i, :, cols])
        hs[:, cols] = (g / (1.0 + jnp.exp(-g)) * u).astype(BF16)

    wide = fd.shape[2]

    @pl.loop(0, n)
    def _(i):
        cols = pl.ds(pl.multiple_of(i * wide, wide), wide)
        part2[:, :, cols] = mm(hs[...], fd[i]).astype(BF16).reshape(m, share, wide)

    part2_copies = mlp_copies(
        lambda peer: part2.at[peer], lambda k: part2_in.at[k - 1], part2_s, part2_r
    )
    total = part2[mj].astype(F32)
    for k, copy in enumerate(part2_copies):
        copy.wait_recv()
        total = total + part2_in[k].astype(F32)
    mixed[...] = (res[...] + total).astype(BF16)

    keep.wait()
    for copy in st_copies:
        copy.wait()
    for copy in tok_copies + part_copies + hid_copies + part2_copies:
        copy.wait_send()
    for copy in w_copies.values():
        copy.wait_send()


def per_device(
    tokens,
    cached_states,
    prompt_lengths,
    accepted,
    owner_slot,
    w_query,
    w_key,
    w_value,
    w_gate_ret,
    w_out,
    w_gate,
    w_up,
    w_down,
):
    requests, heads, dk, dv = cached_states.shape
    n = lax.axis_size("req")
    m = lax.axis_size("mlp")
    share, width = tokens.shape
    rows = requests * DRAFT
    per_peer = requests // n
    gammas = decays(heads, (lax.axis_index("mlp") * heads).astype(F32))
    target_pos = owner_slot // requests * per_peer + owner_slot % per_peer
    ids = jnp.arange(requests, dtype=jnp.int32)
    order = jnp.sum(jnp.where(target_pos[None, :] == ids[:, None], ids[None, :], 0), axis=1)
    kept = accepted.astype(F32)
    old_scale = jnp.power(gammas[None, :], kept[:, None])
    draft_pos = jnp.arange(DRAFT, dtype=F32)
    exponent = kept[:, None] - 1.0 - draft_pos[None, :]
    fold = jnp.where(
        exponent[None] >= 0,
        jnp.power(gammas[:, None, None], jnp.maximum(exponent, 0.0)[None]),
        0.0,
    ).reshape(heads, rows, 1)
    row = jnp.arange(rows, dtype=jnp.int32)
    distance = (row[:, None] - row[None, :]).astype(F32)
    same = (row[:, None] // DRAFT == row[None, :] // DRAFT) & (distance >= 0)
    mask = jnp.where(
        same[None], jnp.power(gammas[:, None, None], jnp.maximum(distance, 0.0)[None]), 0.0
    )
    carry = jnp.power(
        gammas[:, None, None], ((row % DRAFT).astype(F32) + 1.0)[None, :, None]
    )
    half = dk // 2
    frequencies = jnp.exp(-math.log(10000.0) * jnp.arange(half, dtype=F32) / half)
    positions = (
        (prompt_lengths[:, None] + jnp.arange(DRAFT, dtype=jnp.int32)[None, :])
        .astype(F32)
        .reshape(rows, 1)
    )
    angles = positions * frequencies[None, :]
    vmem = pl.BlockSpec(memory_space=pltpu.VMEM)
    smem = pl.BlockSpec(memory_space=pltpu.SMEM)
    hbm = pl.BlockSpec(memory_space=pl.ANY)
    dma = pltpu.SemaphoreType.DMA

    def v(shape, dtype=BF16):
        return pltpu.VMEM(shape, dtype)

    mixed, moved = pl.pallas_call(
        functools.partial(kernel, n, m),
        out_shape=(
            jax.ShapeDtypeStruct((share, width), BF16),
            jax.ShapeDtypeStruct((requests, heads, dk, dv), BF16),
        ),
        in_specs=[smem] * 2 + [vmem] * 5 + [hbm] * 10,
        out_specs=(vmem, hbm),
        scratch_shapes=[
            v(w_query.shape),
            v(w_key.shape),
            v(w_value.shape),
            v(w_gate_ret.shape),
            v(w_out.shape),
            v(cached_states.shape, F32),
            v((n,) + w_gate.shape),
            v((n,) + w_up.shape),
            v((n,) + w_down.shape),
            v((m, share, width)),
            v((rows, width)),
            v((rows, heads * dk)),
            v((requests, DRAFT, heads * dk)),
            v((requests, DRAFT, heads * dv)),
            v((rows, heads * dk)),
            v((rows, heads * dv), F32),
            v((rows, heads * dv), F32),
            v((rows, heads * dv)),
            v((m, share, width)),
            v((m - 1, share, width)),
            v((share, width), F32),
            v((m, share, width)),
            v((rows, w_gate.shape[1])),
            v((m, share, width)),
            v((m - 1, share, width)),
            v(cached_states.shape),
            dma((11,)),
            dma((m - 1,)),
            dma((m - 1,)),
            dma((m - 1,)),
            dma((m - 1,)),
            dma((m - 1,)),
            dma((m - 1,)),
            dma((m - 1,)),
            dma((m - 1,)),
            dma((n - 1, 4)),
            dma((n - 1, 4)),
            dma((n - 1,)),
            dma((n - 1,)),
        ],
        compiler_params=pltpu.CompilerParams(
            collective_id=0, has_side_effects=True, vmem_limit_bytes=60 * 1024 * 1024
        ),
    )(
        order,
        old_scale,
        jnp.cos(angles),
        jnp.sin(angles),
        mask,
        carry,
        fold,
        tokens,
        cached_states,
        w_query,
        w_key,
        w_value,
        w_gate_ret,
        w_out,
        w_gate,
        w_up,
        w_down,
    )
    return (mixed, moved.astype(F32))


def solution(mesh):
    return jax.shard_map(
        per_device,
        mesh=mesh,
        in_specs=(
            P(("req", "mlp"), None),
            P("req", "mlp", None, None),
            P("req"),
            P("req"),
            P("req"),
            P(None, "mlp"),
            P(None, "mlp"),
            P(None, "mlp"),
            P(None, "mlp"),
            P("mlp", None),
            P("req", "mlp"),
            P("req", "mlp"),
            P("mlp", "req"),
        ),
        out_specs=(P(("req", "mlp"), None), P("req", "mlp", None, None)),
        check_vma=False,
    )
```

```python
import functools
import math

import jax
import jax.numpy as jnp
from jax import lax
from jax.experimental import pallas as pl
from jax.experimental.pallas import tpu as pltpu
from jax.sharding import PartitionSpec as P

DRAFT = 16


epsilon = 1e-05


def layer_norm(inputs):
    average = jnp.mean(inputs, axis=-1, keepdims=True)
    centred = inputs - average
    variance = jnp.mean(centred * centred, axis=-1, keepdims=True)
    return centred * lax.rsqrt(variance + epsilon)


MESH = pl.DeviceIdType.MESH
F32 = jnp.float32
BF16 = jnp.bfloat16


def mm(a, b):
    return jnp.dot(a, b, preferred_element_type=F32)


def kernel(
    n,
    m,
    prompt,
    accepted,
    slots,
    tokens,
    states,
    w_query,
    w_key,
    w_value,
    w_gate_ret,
    w_out,
    w_gate,
    w_up,
    w_down,
    mixed,
    moved,
    wq,
    wk,
    wv,
    wgr,
    wo,
    st,
    fg,
    fu,
    fd,
    tok,
    normed,
    rq,
    ksc,
    vals,
    rk_h,
    gated,
    outs,
    joined,
    part,
    part_in,
    res,
    hid,
    hs,
    part2,
    part2_in,
    send_buf,
    load_sem,
    tok_s,
    tok_r,
    part_s,
    part_r,
    hid_s,
    hid_r,
    part2_s,
    part2_r,
    w_s,
    w_r,
    st_s,
    st_r,
):
    me = lax.axis_index("req")
    mj = lax.axis_index("mlp")
    share, width = tokens.shape
    requests, heads, dk, dv = states.shape
    rows = m * share
    half = dk // 2
    per_peer = requests // n
    draft = DRAFT

    barrier = pltpu.get_barrier_semaphore()
    for k in range(1, n):
        pl.semaphore_signal(
            barrier, inc=1, device_id={"req": lax.rem(me + k, n)}, device_id_type=MESH
        )
    for k in range(1, m):
        pl.semaphore_signal(
            barrier, inc=1, device_id={"mlp": lax.rem(mj + k, m)}, device_id_type=MESH
        )

    loads = []
    for a, b in (
        (tokens, tok.at[mj]),
        (w_query, wq),
        (w_key, wk),
        (w_value, wv),
        (w_gate_ret, wgr),
        (states, st),
        (w_out, wo),
        (w_gate, fg.at[me]),
        (w_up, fu.at[me]),
        (w_down, fd.at[me]),
    ):
        copy = pltpu.make_async_copy(a, b, load_sem.at[len(loads)])
        copy.start()
        loads.append(copy)

    pl.semaphore_wait(barrier, n + m - 2)

    def mlp_copies(pick, dst, s, r):
        copies = []
        for k in range(1, m):
            peer = lax.rem(mj + k, m)
            copies.append(
                pltpu.make_async_remote_copy(
                    src_ref=pick(peer),
                    dst_ref=dst(k),
                    send_sem=s.at[k - 1],
                    recv_sem=r.at[k - 1],
                    device_id={"mlp": peer},
                    device_id_type=MESH,
                )
            )
        for copy in copies:
            copy.start()
        return copies

    tok_copies = mlp_copies(lambda peer: tokens, lambda k: tok.at[mj], tok_s, tok_r)

    cut = w_down.shape[0] // 2
    first = pl.ds(0, cut)
    second = pl.ds(cut, cut)

    def pieces(owner, own):
        if own:
            source = (w_gate, w_down.at[first], w_up, w_down.at[second])
        else:
            source = None
        there = (fg.at[owner], fd.at[owner, first], fu.at[owner], fd.at[owner, second])
        return source or there, there

    w_copies = {}

    def send_shard(owner, own, peer, slot, which=(0, 1, 2, 3)):
        source, there = pieces(owner, own)
        for i in which:
            copy = pltpu.make_async_remote_copy(
                src_ref=source[i],
                dst_ref=there[i],
                send_sem=w_s.at[slot, i],
                recv_sem=w_r.at[slot, i],
                device_id={"req": peer},
                device_id_type=MESH,
            )
            copy.start()
            w_copies[slot, i] = copy

    def arrived(slot, which=(0, 1, 2, 3)):
        for i in which:
            w_copies[slot, i].wait_recv()

    def flip(bits):
        out = me
        for bit in (1, 2, 4):
            if bits & bit:
                out = out + bit - 2 * bit * lax.rem(out // bit, 2)
        return out

    if n == 8:
        send_shard(me, True, flip(2), 0)
        send_shard(me, True, flip(4), 1)
        send_shard(me, True, flip(1), 2)
    else:
        for k in range(1, n):
            send_shard(me, True, lax.rem(me + k, n), k - 1)

    row = lax.broadcasted_iota(jnp.int32, (rows, half), 0)
    draft_pos = lax.rem(row, draft)
    start = jnp.zeros((rows, half), jnp.int32)
    kept = jnp.zeros((rows, half), jnp.int32)
    for r in range(requests):
        start = jnp.where(row >= r * draft, prompt[r], start)
        kept = jnp.where(row >= r * draft, accepted[r], kept)
    lane = lax.broadcasted_iota(jnp.int32, (rows, half), 1).astype(F32)
    angles = (start + draft_pos).astype(F32) * jnp.exp(-math.log(10000.0) * lane / half)
    cos_part, sin_part = jnp.cos(angles), jnp.sin(angles)
    exponent = (kept - 1 - draft_pos).astype(F32)
    to = lax.broadcasted_iota(jnp.int32, (rows, rows), 0)
    source = lax.broadcasted_iota(jnp.int32, (rows, rows), 1)
    causal = (to // draft == source // draft) & (to >= source)
    distance = (to - source).astype(F32)

    def log_gamma(h, shape):
        head = jnp.full(shape, mj * heads + h, jnp.int32).astype(F32)
        return jnp.log(1.0 - jnp.exp2(-5.0 - head))

    fold, mask, carry = [], [], []
    for h in range(heads):
        lg = log_gamma(h, (1, half))
        weight = jnp.where(exponent >= 0, jnp.exp(jnp.maximum(exponent, 0.0) * lg), 0.0)
        fold.append(jnp.concatenate([weight, weight], axis=-1))
        carry.append(jnp.exp((draft_pos.astype(F32) + 1.0) * lg)[:, :1])
        mask.append(
            jnp.where(
                causal, jnp.exp(jnp.maximum(distance, 0.0) * log_gamma(h, (1, rows))), 0.0
            )
        )

    loads[0].wait()
    for copy in tok_copies:
        copy.wait_recv()
    normed[...] = layer_norm(tok[...].astype(F32).reshape(rows, width)).astype(BF16)

    def turned(v):
        front, back = v[:, :half], v[:, half:]
        return jnp.concatenate(
            [front * cos_part - back * sin_part, front * sin_part + back * cos_part], axis=-1
        ).astype(BF16)

    loads[1].wait()
    loads[2].wait()
    for h in range(heads):
        cols = pl.ds(h * dk, dk)
        rq[:, cols] = turned(mm(normed[...], wq[:, cols]))
        rk = turned(mm(normed[...], wk[:, cols]) * (1.0 / math.sqrt(dk)))
        rk_h[:, cols] = rk
        ksc[:, :, cols] = (
            (rk.astype(F32) * fold[h]).astype(BF16).reshape(requests, draft, dk)
        )
    loads[3].wait()
    for h in range(heads):
        cols = pl.ds(h * dv, dv)
        vals[:, :, cols] = mm(normed[...], wv[:, cols]).astype(BF16).reshape(
            requests, draft, dv
        )
    loads[5].wait()

    st_copies = []

    def fresh(p):
        r = 0
        for q in range(requests):
            slot = slots[q]
            place = slot // requests * per_peer + lax.rem(slot, per_peer)
            r = jnp.where(place == p, q, r)
        count = jnp.full((1, dv), accepted[r], jnp.int32).astype(F32)
        for h in range(heads):
            old_scale = jnp.exp(count * log_gamma(h, (1, dv)))
            update = lax.dot_general(
                ksc[r, :, h * dk : (h + 1) * dk],
                vals[r, :, h * dv : (h + 1) * dv],
                (((0,), (0,)), ((), ())),
                preferred_element_type=F32,
            )
            send_buf[p, h] = (old_scale * st[r, h] + update).astype(BF16)

    pl.loop(0, requests)(fresh)
    mine = pl.ds(me * per_peer, per_peer)
    for k in range(1, n):
        peer = lax.rem(me + k, n)
        copy = pltpu.make_async_remote_copy(
            src_ref=send_buf.at[pl.ds(peer * per_peer, per_peer)],
            dst_ref=moved.at[mine],
            send_sem=st_s.at[k - 1],
            recv_sem=st_r.at[k - 1],
            device_id={"req": peer},
            device_id_type=MESH,
        )
        copy.start()
        st_copies.append(copy)
    keep = pltpu.make_async_copy(send_buf.at[mine], moved.at[mine], load_sem.at[10])
    keep.start()

    loads[4].wait()
    for h in range(heads):
        cols = pl.ds(h * dv, dv)
        g = mm(normed[...], wgr[:, cols])
        gated[:, cols] = g / (1.0 + jnp.exp(-g))

    @pl.loop(0, requests)
    def _(r):
        here = pl.ds(pl.multiple_of(r * draft, draft), draft)
        for h in range(heads):
            outs[here, h * dv : (h + 1) * dv] = mm(
                rq[here, h * dk : (h + 1) * dk], st[r, h].astype(BF16)
            )

    for h in range(heads):
        cols = pl.ds(h * dk, dk)
        vcols = pl.ds(h * dv, dv)
        scores = lax.dot_general(
            rq[:, cols], rk_h[:, cols], (((1,), (1,)), ((), ())), preferred_element_type=F32
        )
        weights = (scores * mask[h]).astype(BF16)
        out = mm(weights, vals[:, :, vcols].reshape(rows, dv)) + outs[:, vcols] * carry[h]
        joined[:, vcols] = (layer_norm(out) * gated[:, vcols]).astype(BF16)

    loads[6].wait()
    step = min(512, width)

    @pl.loop(0, width // step)
    def _(c):
        cols = pl.ds(pl.multiple_of(c * step, step), step)
        part[:, :, cols] = mm(joined[...], wo[:, cols]).astype(BF16).reshape(m, share, step)

    part_copies = mlp_copies(
        lambda peer: part.at[peer], lambda k: part_in.at[k - 1], part_s, part_r
    )

    if n == 8:
        arrived(0)
        send_shard(flip(2), False, flip(4), 3, (0, 1))
        arrived(1)
        send_shard(flip(4), False, flip(2), 3, (2, 3))
        send_shard(flip(2), False, flip(1), 4)
        send_shard(flip(4), False, flip(1), 5)

    total = part[mj].astype(F32)
    for k, copy in enumerate(part_copies):
        copy.wait_recv()
        total = total + part_in[k].astype(F32)
    residual = tok[mj].astype(F32) + total
    res[...] = residual
    hid[mj] = layer_norm(residual).astype(BF16)
    hid_copies = mlp_copies(lambda peer: hid.at[mj], lambda k: hid.at[mj], hid_s, hid_r)

    if n == 8:
        arrived(3)
        send_shard(flip(6), False, flip(1), 6)
        last = (2, 4, 5, 6)
    else:
        last = tuple(range(n - 1))
    for copy in hid_copies:
        copy.wait_recv()
    for slot in last:
        arrived(slot)
    for copy in loads[7:]:
        copy.wait()

    rows_in = fg.shape[1]
    inner = fg.shape[2]
    tile = min(256, inner)

    @pl.loop(0, inner // tile)
    def _(c):
        cols = pl.ds(pl.multiple_of(c * tile, tile), tile)
        g = jnp.zeros((rows, tile), F32)
        u = jnp.zeros((rows, tile), F32)
        for i in range(n):
            a = hid[:, :, i * rows_in : (i + 1) * rows_in].reshape(rows, rows_in)
            g = g + mm(a, fg[i, :, cols])
            u = u + mm(a, fu[i, :, cols])
        hs[:, cols] = (g / (1.0 + jnp.exp(-g)) * u).astype(BF16)

    wide = fd.shape[2]

    @pl.loop(0, n)
    def _(i):
        cols = pl.ds(pl.multiple_of(i * wide, wide), wide)
        part2[:, :, cols] = mm(hs[...], fd[i]).astype(BF16).reshape(m, share, wide)

    part2_copies = mlp_copies(
        lambda peer: part2.at[peer], lambda k: part2_in.at[k - 1], part2_s, part2_r
    )
    total = part2[mj].astype(F32)
    for k, copy in enumerate(part2_copies):
        copy.wait_recv()
        total = total + part2_in[k].astype(F32)
    mixed[...] = (res[...] + total).astype(BF16)

    keep.wait()
    for copy in st_copies:
        copy.wait()
    for copy in tok_copies + part_copies + hid_copies + part2_copies:
        copy.wait_send()
    for copy in w_copies.values():
        copy.wait_send()


def per_device(
    tokens,
    cached_states,
    prompt_lengths,
    accepted,
    owner_slot,
    w_query,
    w_key,
    w_value,
    w_gate_ret,
    w_out,
    w_gate,
    w_up,
    w_down,
):
    requests, heads, dk, dv = cached_states.shape
    n = lax.axis_size("req")
    m = lax.axis_size("mlp")
    share, width = tokens.shape
    rows = requests * DRAFT
    vmem = pl.BlockSpec(memory_space=pltpu.VMEM)
    smem = pl.BlockSpec(memory_space=pltpu.SMEM)
    hbm = pl.BlockSpec(memory_space=pl.ANY)
    dma = pltpu.SemaphoreType.DMA

    def v(shape, dtype=BF16):
        return pltpu.VMEM(shape, dtype)

    mixed, moved = pl.pallas_call(
        functools.partial(kernel, n, m),
        out_shape=(
            jax.ShapeDtypeStruct((share, width), BF16),
            jax.ShapeDtypeStruct((requests, heads, dk, dv), BF16),
        ),
        in_specs=[smem] * 3 + [hbm] * 10,
        out_specs=(vmem, hbm),
        scratch_shapes=[
            v(w_query.shape),
            v(w_key.shape),
            v(w_value.shape),
            v(w_gate_ret.shape),
            v(w_out.shape),
            v(cached_states.shape, F32),
            v((n,) + w_gate.shape),
            v((n,) + w_up.shape),
            v((n,) + w_down.shape),
            v((m, share, width)),
            v((rows, width)),
            v((rows, heads * dk)),
            v((requests, DRAFT, heads * dk)),
            v((requests, DRAFT, heads * dv)),
            v((rows, heads * dk)),
            v((rows, heads * dv), F32),
            v((rows, heads * dv), F32),
            v((rows, heads * dv)),
            v((m, share, width)),
            v((m - 1, share, width)),
            v((share, width), F32),
            v((m, share, width)),
            v((rows, w_gate.shape[1])),
            v((m, share, width)),
            v((m - 1, share, width)),
            v(cached_states.shape),
            dma((11,)),
            dma((m - 1,)),
            dma((m - 1,)),
            dma((m - 1,)),
            dma((m - 1,)),
            dma((m - 1,)),
            dma((m - 1,)),
            dma((m - 1,)),
            dma((m - 1,)),
            dma((n - 1, 4)),
            dma((n - 1, 4)),
            dma((n - 1,)),
            dma((n - 1,)),
        ],
        compiler_params=pltpu.CompilerParams(
            collective_id=0, has_side_effects=True, vmem_limit_bytes=60 * 1024 * 1024
        ),
    )(
        prompt_lengths,
        accepted,
        owner_slot,
        tokens,
        cached_states,
        w_query,
        w_key,
        w_value,
        w_gate_ret,
        w_out,
        w_gate,
        w_up,
        w_down,
    )
    return (mixed, moved.astype(F32))


def solution(mesh):
    return jax.shard_map(
        per_device,
        mesh=mesh,
        in_specs=(
            P(("req", "mlp"), None),
            P("req", "mlp", None, None),
            P("req"),
            P("req"),
            P("req"),
            P(None, "mlp"),
            P(None, "mlp"),
            P(None, "mlp"),
            P(None, "mlp"),
            P("mlp", None),
            P("req", "mlp"),
            P("req", "mlp"),
            P("mlp", "req"),
        ),
        out_specs=(P(("req", "mlp"), None), P("req", "mlp", None, None)),
        check_vma=False,
    )
```

```python
import functools
import math

import jax
import jax.numpy as jnp
from jax import lax
from jax.experimental import pallas as pl
from jax.experimental.pallas import tpu as pltpu
from jax.sharding import PartitionSpec as P

DRAFT = 16


epsilon = 1e-05


def layer_norm(inputs):
    average = jnp.mean(inputs, axis=-1, keepdims=True)
    centred = inputs - average
    variance = jnp.mean(centred * centred, axis=-1, keepdims=True)
    return centred * lax.rsqrt(variance + epsilon)


MESH = pl.DeviceIdType.MESH
F32 = jnp.float32
BF16 = jnp.bfloat16


def mm(a, b):
    return jnp.dot(a, b, preferred_element_type=F32)


def kernel(
    n,
    m,
    prompt,
    accepted,
    slots,
    tokens,
    states,
    w_query,
    w_key,
    w_value,
    w_gate_ret,
    w_out,
    w_gate,
    w_up,
    w_down,
    mixed,
    moved,
    wq,
    wk,
    wv,
    wgr,
    wo,
    st,
    fg,
    fu,
    fd,
    tok,
    normed,
    rq,
    ksc,
    vals,
    rk_h,
    gated,
    outs,
    joined,
    part,
    part_in,
    res,
    hid,
    hs,
    part2,
    part2_in,
    send_buf,
    load_sem,
    tok_s,
    tok_r,
    part_s,
    part_r,
    hid_s,
    hid_r,
    part2_s,
    part2_r,
    w_s,
    w_r,
    st_s,
    st_r,
):
    me = lax.axis_index("req")
    mj = lax.axis_index("mlp")
    share, width = tokens.shape
    requests, heads, dk, dv = states.shape
    rows = m * share
    half = dk // 2
    per_peer = requests // n
    draft = DRAFT

    barrier = pltpu.get_barrier_semaphore()
    for k in range(1, n):
        pl.semaphore_signal(
            barrier, inc=1, device_id={"req": lax.rem(me + k, n)}, device_id_type=MESH
        )
    for k in range(1, m):
        pl.semaphore_signal(
            barrier, inc=1, device_id={"mlp": lax.rem(mj + k, m)}, device_id_type=MESH
        )

    loads = []
    for a, b in (
        (tokens, tok.at[mj]),
        (w_query, wq),
        (w_key, wk),
        (w_value, wv),
        (w_gate_ret, wgr),
        (states, st),
        (w_out, wo),
        (w_gate, fg.at[me]),
        (w_up, fu.at[me]),
        (w_down, fd.at[me]),
    ):
        copy = pltpu.make_async_copy(a, b, load_sem.at[len(loads)])
        copy.start()
        loads.append(copy)

    pl.semaphore_wait(barrier, n + m - 2)

    def mlp_copies(pick, dst, s, r):
        copies = []
        for k in range(1, m):
            peer = lax.rem(mj + k, m)
            copies.append(
                pltpu.make_async_remote_copy(
                    src_ref=pick(peer),
                    dst_ref=dst(k),
                    send_sem=s.at[k - 1],
                    recv_sem=r.at[k - 1],
                    device_id={"mlp": peer},
                    device_id_type=MESH,
                )
            )
        for copy in copies:
            copy.start()
        return copies

    tok_copies = mlp_copies(lambda peer: tokens, lambda k: tok.at[mj], tok_s, tok_r)

    cut = w_down.shape[0] // 2
    first = pl.ds(0, cut)
    second = pl.ds(cut, cut)

    def pieces(owner, own):
        if own:
            source = (w_gate, w_down.at[first], w_up, w_down.at[second])
        else:
            source = None
        there = (fg.at[owner], fd.at[owner, first], fu.at[owner], fd.at[owner, second])
        return source or there, there

    w_copies = {}

    def send_shard(owner, own, peer, slot, which=(0, 1, 2, 3)):
        source, there = pieces(owner, own)
        for i in which:
            copy = pltpu.make_async_remote_copy(
                src_ref=source[i],
                dst_ref=there[i],
                send_sem=w_s.at[slot, i],
                recv_sem=w_r.at[slot, i],
                device_id={"req": peer},
                device_id_type=MESH,
            )
            copy.start()
            w_copies[slot, i] = copy

    def arrived(slot, which=(0, 1, 2, 3)):
        for i in which:
            w_copies[slot, i].wait_recv()

    def flip(bits):
        out = me
        for bit in (1, 2, 4):
            if bits & bit:
                out = out + bit - 2 * bit * lax.rem(out // bit, 2)
        return out

    if n == 8:
        send_shard(me, True, flip(2), 0)
        send_shard(me, True, flip(4), 1)
        send_shard(me, True, flip(1), 2)
    else:
        for k in range(1, n):
            send_shard(me, True, lax.rem(me + k, n), k - 1)

    row = lax.broadcasted_iota(jnp.int32, (rows, half), 0)
    draft_pos = lax.rem(row, draft)
    start = jnp.zeros((rows, half), jnp.int32)
    kept = jnp.zeros((rows, half), jnp.int32)
    for r in range(requests):
        start = jnp.where(row >= r * draft, prompt[r], start)
        kept = jnp.where(row >= r * draft, accepted[r], kept)
    lane = lax.broadcasted_iota(jnp.int32, (rows, half), 1).astype(F32)
    angles = (start + draft_pos).astype(F32) * jnp.exp(-math.log(10000.0) * lane / half)
    cos_part, sin_part = jnp.cos(angles), jnp.sin(angles)
    exponent = (kept - 1 - draft_pos).astype(F32)
    to = lax.broadcasted_iota(jnp.int32, (rows, rows), 0)
    source = lax.broadcasted_iota(jnp.int32, (rows, rows), 1)
    causal = (to // draft == source // draft) & (to >= source)
    distance = (to - source).astype(F32)

    def log_gamma(h, shape):
        head = jnp.full(shape, mj * heads + h, jnp.int32).astype(F32)
        return jnp.log(1.0 - jnp.exp2(-5.0 - head))

    fold, mask, carry = [], [], []
    for h in range(heads):
        lg = log_gamma(h, (1, half))
        weight = jnp.where(exponent >= 0, jnp.exp(jnp.maximum(exponent, 0.0) * lg), 0.0)
        fold.append(jnp.concatenate([weight, weight], axis=-1))
        carry.append(jnp.exp((draft_pos.astype(F32) + 1.0) * lg)[:, :1])
        mask.append(
            jnp.where(
                causal, jnp.exp(jnp.maximum(distance, 0.0) * log_gamma(h, (1, rows))), 0.0
            )
        )

    loads[0].wait()
    for copy in tok_copies:
        copy.wait_recv()
    normed[...] = layer_norm(tok[...].astype(F32).reshape(rows, width)).astype(BF16)

    def turned(v):
        front, back = v[:, :half], v[:, half:]
        return jnp.concatenate(
            [front * cos_part - back * sin_part, front * sin_part + back * cos_part], axis=-1
        ).astype(BF16)

    loads[1].wait()
    loads[2].wait()
    for h in range(heads):
        cols = pl.ds(h * dk, dk)
        rq[:, cols] = turned(mm(normed[...], wq[:, cols]))
        rk = turned(mm(normed[...], wk[:, cols]) * (1.0 / math.sqrt(dk)))
        rk_h[:, cols] = rk
        ksc[:, :, cols] = (
            (rk.astype(F32) * fold[h]).astype(BF16).reshape(requests, draft, dk)
        )
    loads[3].wait()
    for h in range(heads):
        cols = pl.ds(h * dv, dv)
        vals[:, :, cols] = mm(normed[...], wv[:, cols]).astype(BF16).reshape(
            requests, draft, dv
        )
    loads[5].wait()

    loads[4].wait()
    for h in range(heads):
        cols = pl.ds(h * dv, dv)
        g = mm(normed[...], wgr[:, cols])
        gated[:, cols] = g / (1.0 + jnp.exp(-g))

    @pl.loop(0, requests)
    def _(r):
        here = pl.ds(pl.multiple_of(r * draft, draft), draft)
        for h in range(heads):
            outs[here, h * dv : (h + 1) * dv] = mm(
                rq[here, h * dk : (h + 1) * dk], st[r, h].astype(BF16)
            )

    for h in range(heads):
        cols = pl.ds(h * dk, dk)
        vcols = pl.ds(h * dv, dv)
        scores = lax.dot_general(
            rq[:, cols], rk_h[:, cols], (((1,), (1,)), ((), ())), preferred_element_type=F32
        )
        weights = (scores * mask[h]).astype(BF16)
        out = mm(weights, vals[:, :, vcols].reshape(rows, dv)) + outs[:, vcols] * carry[h]
        joined[:, vcols] = (layer_norm(out) * gated[:, vcols]).astype(BF16)

    loads[6].wait()
    step = min(512, width)

    @pl.loop(0, width // step)
    def _(c):
        cols = pl.ds(pl.multiple_of(c * step, step), step)
        part[:, :, cols] = mm(joined[...], wo[:, cols]).astype(BF16).reshape(m, share, step)

    part_copies = mlp_copies(
        lambda peer: part.at[peer], lambda k: part_in.at[k - 1], part_s, part_r
    )

    if n == 8:
        arrived(0)
        send_shard(flip(2), False, flip(4), 3, (0, 1))
        arrived(1)
        send_shard(flip(4), False, flip(2), 3, (2, 3))
        send_shard(flip(2), False, flip(1), 4)
        send_shard(flip(4), False, flip(1), 5)

    st_copies = []

    def fresh(p):
        r = 0
        for q in range(requests):
            slot = slots[q]
            place = slot // requests * per_peer + lax.rem(slot, per_peer)
            r = jnp.where(place == p, q, r)
        count = jnp.full((1, dv), accepted[r], jnp.int32).astype(F32)
        for h in range(heads):
            old_scale = jnp.exp(count * log_gamma(h, (1, dv)))
            update = lax.dot_general(
                ksc[r, :, h * dk : (h + 1) * dk],
                vals[r, :, h * dv : (h + 1) * dv],
                (((0,), (0,)), ((), ())),
                preferred_element_type=F32,
            )
            send_buf[p, h] = (old_scale * st[r, h] + update).astype(BF16)

    pl.loop(0, requests)(fresh)

    total = part[mj].astype(F32)
    for k, copy in enumerate(part_copies):
        copy.wait_recv()
        total = total + part_in[k].astype(F32)
    residual = tok[mj].astype(F32) + total
    res[...] = residual
    hid[mj] = layer_norm(residual).astype(BF16)
    hid_copies = mlp_copies(lambda peer: hid.at[mj], lambda k: hid.at[mj], hid_s, hid_r)

    if n == 8:
        arrived(3)
        send_shard(flip(6), False, flip(1), 6)
        last = (2, 4, 5, 6)
    else:
        last = tuple(range(n - 1))

    mine = pl.ds(me * per_peer, per_peer)
    for k in range(1, n):
        peer = lax.rem(me + k, n)
        copy = pltpu.make_async_remote_copy(
            src_ref=send_buf.at[pl.ds(peer * per_peer, per_peer)],
            dst_ref=moved.at[mine],
            send_sem=st_s.at[k - 1],
            recv_sem=st_r.at[k - 1],
            device_id={"req": peer},
            device_id_type=MESH,
        )
        copy.start()
        st_copies.append(copy)
    keep = pltpu.make_async_copy(send_buf.at[mine], moved.at[mine], load_sem.at[10])
    keep.start()
    for copy in hid_copies:
        copy.wait_recv()
    for slot in last:
        arrived(slot)
    for copy in loads[7:]:
        copy.wait()

    rows_in = fg.shape[1]
    inner = fg.shape[2]
    tile = min(256, inner)

    @pl.loop(0, inner // tile)
    def _(c):
        cols = pl.ds(pl.multiple_of(c * tile, tile), tile)
        g = jnp.zeros((rows, tile), F32)
        u = jnp.zeros((rows, tile), F32)
        for i in range(n):
            a = hid[:, :, i * rows_in : (i + 1) * rows_in].reshape(rows, rows_in)
            g = g + mm(a, fg[i, :, cols])
            u = u + mm(a, fu[i, :, cols])
        hs[:, cols] = (g / (1.0 + jnp.exp(-g)) * u).astype(BF16)

    wide = fd.shape[2]

    @pl.loop(0, n)
    def _(i):
        cols = pl.ds(pl.multiple_of(i * wide, wide), wide)
        part2[:, :, cols] = mm(hs[...], fd[i]).astype(BF16).reshape(m, share, wide)

    part2_copies = mlp_copies(
        lambda peer: part2.at[peer], lambda k: part2_in.at[k - 1], part2_s, part2_r
    )
    total = part2[mj].astype(F32)
    for k, copy in enumerate(part2_copies):
        copy.wait_recv()
        total = total + part2_in[k].astype(F32)
    mixed[...] = (res[...] + total).astype(BF16)

    keep.wait()
    for copy in st_copies:
        copy.wait()
    for copy in tok_copies + part_copies + hid_copies + part2_copies:
        copy.wait_send()
    for copy in w_copies.values():
        copy.wait_send()


def widen(x, out):
    out[...] = x[...].astype(F32)


def per_device(
    tokens,
    cached_states,
    prompt_lengths,
    accepted,
    owner_slot,
    w_query,
    w_key,
    w_value,
    w_gate_ret,
    w_out,
    w_gate,
    w_up,
    w_down,
):
    requests, heads, dk, dv = cached_states.shape
    n = lax.axis_size("req")
    m = lax.axis_size("mlp")
    share, width = tokens.shape
    rows = requests * DRAFT
    vmem = pl.BlockSpec(memory_space=pltpu.VMEM)
    smem = pl.BlockSpec(memory_space=pltpu.SMEM)
    hbm = pl.BlockSpec(memory_space=pl.ANY)
    dma = pltpu.SemaphoreType.DMA

    def v(shape, dtype=BF16):
        return pltpu.VMEM(shape, dtype)

    mixed, moved = pl.pallas_call(
        functools.partial(kernel, n, m),
        out_shape=(
            jax.ShapeDtypeStruct((share, width), BF16),
            jax.ShapeDtypeStruct((requests, heads, dk, dv), BF16),
        ),
        in_specs=[smem] * 3 + [hbm] * 10,
        out_specs=(vmem, hbm),
        scratch_shapes=[
            v(w_query.shape),
            v(w_key.shape),
            v(w_value.shape),
            v(w_gate_ret.shape),
            v(w_out.shape),
            v(cached_states.shape, F32),
            v((n,) + w_gate.shape),
            v((n,) + w_up.shape),
            v((n,) + w_down.shape),
            v((m, share, width)),
            v((rows, width)),
            v((rows, heads * dk)),
            v((requests, DRAFT, heads * dk)),
            v((requests, DRAFT, heads * dv)),
            v((rows, heads * dk)),
            v((rows, heads * dv), F32),
            v((rows, heads * dv), F32),
            v((rows, heads * dv)),
            v((m, share, width)),
            v((m - 1, share, width)),
            v((share, width), F32),
            v((m, share, width)),
            v((rows, w_gate.shape[1])),
            v((m, share, width)),
            v((m - 1, share, width)),
            v(cached_states.shape),
            dma((11,)),
            dma((m - 1,)),
            dma((m - 1,)),
            dma((m - 1,)),
            dma((m - 1,)),
            dma((m - 1,)),
            dma((m - 1,)),
            dma((m - 1,)),
            dma((m - 1,)),
            dma((n - 1, 4)),
            dma((n - 1, 4)),
            dma((n - 1,)),
            dma((n - 1,)),
        ],
        compiler_params=pltpu.CompilerParams(
            collective_id=0, has_side_effects=True, vmem_limit_bytes=60 * 1024 * 1024
        ),
    )(
        prompt_lengths,
        accepted,
        owner_slot,
        tokens,
        cached_states,
        w_query,
        w_key,
        w_value,
        w_gate_ret,
        w_out,
        w_gate,
        w_up,
        w_down,
    )
    block = pl.BlockSpec((1, 1, dk, dv), lambda r, h: (r, h, 0, 0))
    new_states = pl.pallas_call(
        widen,
        out_shape=jax.ShapeDtypeStruct(cached_states.shape, F32),
        grid=(requests, heads),
        in_specs=[block],
        out_specs=block,
    )(moved)
    return (mixed, new_states)


def solution(mesh):
    return jax.shard_map(
        per_device,
        mesh=mesh,
        in_specs=(
            P(("req", "mlp"), None),
            P("req", "mlp", None, None),
            P("req"),
            P("req"),
            P("req"),
            P(None, "mlp"),
            P(None, "mlp"),
            P(None, "mlp"),
            P(None, "mlp"),
            P("mlp", None),
            P("req", "mlp"),
            P("req", "mlp"),
            P("mlp", "req"),
        ),
        out_specs=(P(("req", "mlp"), None), P("req", "mlp", None, None)),
        check_vma=False,
    )
```

```python
import functools
import math

import jax
import jax.numpy as jnp
from jax import lax
from jax.experimental import pallas as pl
from jax.experimental.pallas import tpu as pltpu
from jax.sharding import PartitionSpec as P

DRAFT = 16


epsilon = 1e-05


def layer_norm(inputs):
    average = jnp.mean(inputs, axis=-1, keepdims=True)
    centred = inputs - average
    variance = jnp.mean(centred * centred, axis=-1, keepdims=True)
    return centred * lax.rsqrt(variance + epsilon)


MESH = pl.DeviceIdType.MESH
F32 = jnp.float32
BF16 = jnp.bfloat16


def mm(a, b):
    return jnp.dot(a, b, preferred_element_type=F32)


def kernel(
    n,
    m,
    prompt,
    accepted,
    slots,
    tokens,
    states,
    w_query,
    w_key,
    w_value,
    w_gate_ret,
    w_out,
    w_gate,
    w_up,
    w_down,
    mixed,
    moved,
    wq,
    wk,
    wv,
    wgr,
    wo,
    st,
    fg,
    fu,
    fd,
    tok,
    normed,
    rq,
    ksc,
    vals,
    rk_h,
    gated,
    outs,
    joined,
    part,
    part_in,
    res,
    hid,
    hs,
    part2,
    part2_in,
    send_buf,
    hx,
    hy,
    sx,
    sy,
    rx,
    ry,
    og,
    ou,
    load_sem,
    tok_s,
    tok_r,
    part_s,
    part_r,
    hid_s,
    hid_r,
    part2_s,
    part2_r,
    w_s,
    w_r,
    st_s,
    st_r,
    x_s,
    x_r,
):
    me = lax.axis_index("req")
    mj = lax.axis_index("mlp")
    share, width = tokens.shape
    requests, heads, dk, dv = states.shape
    rows = m * share
    half = dk // 2
    per_peer = requests // n
    draft = DRAFT

    barrier = pltpu.get_barrier_semaphore()
    for k in range(1, n):
        pl.semaphore_signal(
            barrier, inc=1, device_id={"req": lax.rem(me + k, n)}, device_id_type=MESH
        )
    for k in range(1, m):
        pl.semaphore_signal(
            barrier, inc=1, device_id={"mlp": lax.rem(mj + k, m)}, device_id_type=MESH
        )

    loads = []
    for a, b in (
        (tokens, tok.at[mj]),
        (w_query, wq),
        (w_key, wk),
        (w_value, wv),
        (w_gate_ret, wgr),
        (states, st),
        (w_out, wo),
        (w_gate, fg.at[me]),
        (w_up, fu.at[me]),
        (w_down, fd.at[me]),
    ):
        copy = pltpu.make_async_copy(a, b, load_sem.at[len(loads)])
        copy.start()
        loads.append(copy)

    pl.semaphore_wait(barrier, n + m - 2)

    def mlp_copies(pick, dst, s, r):
        copies = []
        for k in range(1, m):
            peer = lax.rem(mj + k, m)
            copies.append(
                pltpu.make_async_remote_copy(
                    src_ref=pick(peer),
                    dst_ref=dst(k),
                    send_sem=s.at[k - 1],
                    recv_sem=r.at[k - 1],
                    device_id={"mlp": peer},
                    device_id_type=MESH,
                )
            )
        for copy in copies:
            copy.start()
        return copies

    tok_copies = mlp_copies(lambda peer: tokens, lambda k: tok.at[mj], tok_s, tok_r)

    cut = w_down.shape[0] // 2
    edge = w_gate.shape[1] // 2
    both = pl.ds(0, w_gate.shape[0])
    cut_of = {
        "g": (w_gate, fg, ()),
        "u": (w_up, fu, ()),
        "ga": (w_gate, fg, (both, pl.ds(0, edge))),
        "gb": (w_gate, fg, (both, pl.ds(edge, edge))),
        "ua": (w_up, fu, (both, pl.ds(0, edge))),
        "ub": (w_up, fu, (both, pl.ds(edge, edge))),
        "d0": (w_down, fd, (pl.ds(0, cut),)),
        "d1": (w_down, fd, (pl.ds(cut, cut),)),
    }

    w_copies = {}

    def send_shard(owner, own, peer, slot, names=("g", "u", "d0", "d1"), at=0):
        for i, name in enumerate(names):
            given, held, where = cut_of[name]
            there = held.at[(owner,) + where]
            copy = pltpu.make_async_remote_copy(
                src_ref=(given.at[where] if where else given) if own else there,
                dst_ref=there,
                send_sem=w_s.at[slot, at + i],
                recv_sem=w_r.at[slot, at + i],
                device_id={"req": peer},
                device_id_type=MESH,
            )
            copy.start()
            w_copies[slot, at + i] = copy

    def arrived(slot):
        for (at, _), copy in w_copies.items():
            if at == slot:
                copy.wait_recv()

    def flip(bits):
        out = me
        for bit in (1, 2, 4):
            if bits & bit:
                out = out + bit - 2 * bit * lax.rem(out // bit, 2)
        return out

    if n == 8:
        side_x = ("gb", "ub", "d0", "d1")
        side_y = ("ga", "ua", "d0", "d1")
        send_shard(me, True, flip(2), 0, side_x)
        send_shard(me, True, flip(4), 1, side_y)
        send_shard(me, True, flip(1), 2)
    else:
        for k in range(1, n):
            send_shard(me, True, lax.rem(me + k, n), k - 1)

    row = lax.broadcasted_iota(jnp.int32, (rows, half), 0)
    draft_pos = lax.rem(row, draft)
    start = jnp.zeros((rows, half), jnp.int32)
    kept = jnp.zeros((rows, half), jnp.int32)
    for r in range(requests):
        start = jnp.where(row >= r * draft, prompt[r], start)
        kept = jnp.where(row >= r * draft, accepted[r], kept)
    lane = lax.broadcasted_iota(jnp.int32, (rows, half), 1).astype(F32)
    angles = (start + draft_pos).astype(F32) * jnp.exp(-math.log(10000.0) * lane / half)
    cos_part, sin_part = jnp.cos(angles), jnp.sin(angles)
    exponent = (kept - 1 - draft_pos).astype(F32)
    to = lax.broadcasted_iota(jnp.int32, (rows, rows), 0)
    source = lax.broadcasted_iota(jnp.int32, (rows, rows), 1)
    causal = (to // draft == source // draft) & (to >= source)
    distance = (to - source).astype(F32)

    def log_gamma(h, shape):
        head = jnp.full(shape, mj * heads + h, jnp.int32).astype(F32)
        return jnp.log(1.0 - jnp.exp2(-5.0 - head))

    fold, mask, carry = [], [], []
    for h in range(heads):
        lg = log_gamma(h, (1, half))
        weight = jnp.where(exponent >= 0, jnp.exp(jnp.maximum(exponent, 0.0) * lg), 0.0)
        fold.append(jnp.concatenate([weight, weight], axis=-1))
        carry.append(jnp.exp((draft_pos.astype(F32) + 1.0) * lg)[:, :1])
        mask.append(
            jnp.where(
                causal, jnp.exp(jnp.maximum(distance, 0.0) * log_gamma(h, (1, rows))), 0.0
            )
        )

    loads[0].wait()
    for copy in tok_copies:
        copy.wait_recv()
    normed[...] = layer_norm(tok[...].astype(F32).reshape(rows, width)).astype(BF16)

    def turned(v):
        front, back = v[:, :half], v[:, half:]
        return jnp.concatenate(
            [front * cos_part - back * sin_part, front * sin_part + back * cos_part], axis=-1
        ).astype(BF16)

    loads[1].wait()
    loads[2].wait()
    for h in range(heads):
        cols = pl.ds(h * dk, dk)
        rq[:, cols] = turned(mm(normed[...], wq[:, cols]))
        rk = turned(mm(normed[...], wk[:, cols]) * (1.0 / math.sqrt(dk)))
        rk_h[:, cols] = rk
        ksc[:, :, cols] = (
            (rk.astype(F32) * fold[h]).astype(BF16).reshape(requests, draft, dk)
        )
    loads[3].wait()
    for h in range(heads):
        cols = pl.ds(h * dv, dv)
        vals[:, :, cols] = mm(normed[...], wv[:, cols]).astype(BF16).reshape(
            requests, draft, dv
        )
    loads[5].wait()

    st_copies = []

    def fresh(p):
        r = 0
        for q in range(requests):
            slot = slots[q]
            place = slot // requests * per_peer + lax.rem(slot, per_peer)
            r = jnp.where(place == p, q, r)
        count = jnp.full((1, dv), accepted[r], jnp.int32).astype(F32)
        for h in range(heads):
            old_scale = jnp.exp(count * log_gamma(h, (1, dv)))
            update = lax.dot_general(
                ksc[r, :, h * dk : (h + 1) * dk],
                vals[r, :, h * dv : (h + 1) * dv],
                (((0,), (0,)), ((), ())),
                preferred_element_type=F32,
            )
            send_buf[p, h] = (old_scale * st[r, h] + update).astype(BF16)

    pl.loop(0, requests)(fresh)
    mine = pl.ds(me * per_peer, per_peer)

    def send_states(peer, slot):
        copy = pltpu.make_async_remote_copy(
            src_ref=send_buf.at[pl.ds(peer * per_peer, per_peer)],
            dst_ref=moved.at[mine],
            send_sem=st_s.at[slot],
            recv_sem=st_r.at[slot],
            device_id={"req": peer},
            device_id_type=MESH,
        )
        copy.start()
        st_copies.append(copy)

    if n == 8:
        for bits in (2, 4, 6, 3, 5, 1):
            send_states(flip(bits), bits - 1)
    else:
        for k in range(1, n):
            send_states(lax.rem(me + k, n), k - 1)
    keep = pltpu.make_async_copy(send_buf.at[mine], moved.at[mine], load_sem.at[10])
    keep.start()

    loads[4].wait()
    for h in range(heads):
        cols = pl.ds(h * dv, dv)
        g = mm(normed[...], wgr[:, cols])
        gated[:, cols] = g / (1.0 + jnp.exp(-g))

    @pl.loop(0, requests)
    def _(r):
        here = pl.ds(pl.multiple_of(r * draft, draft), draft)
        for h in range(heads):
            outs[here, h * dv : (h + 1) * dv] = mm(
                rq[here, h * dk : (h + 1) * dk], st[r, h].astype(BF16)
            )

    for h in range(heads):
        cols = pl.ds(h * dk, dk)
        vcols = pl.ds(h * dv, dv)
        scores = lax.dot_general(
            rq[:, cols], rk_h[:, cols], (((1,), (1,)), ((), ())), preferred_element_type=F32
        )
        weights = (scores * mask[h]).astype(BF16)
        out = mm(weights, vals[:, :, vcols].reshape(rows, dv)) + outs[:, vcols] * carry[h]
        joined[:, vcols] = (layer_norm(out) * gated[:, vcols]).astype(BF16)

    loads[6].wait()
    step = min(512, width)

    @pl.loop(0, width // step)
    def _(c):
        cols = pl.ds(pl.multiple_of(c * step, step), step)
        part[:, :, cols] = mm(joined[...], wo[:, cols]).astype(BF16).reshape(m, share, step)

    part_copies = mlp_copies(
        lambda peer: part.at[peer], lambda k: part_in.at[k - 1], part_s, part_r
    )

    if n == 8:
        arrived(0)
        send_shard(flip(2), False, flip(4), 3, ("d0",))
        arrived(1)
        send_shard(flip(4), False, flip(2), 3, ("d1",), 1)
        send_shard(flip(2), False, flip(1), 4, side_x)
        send_shard(flip(4), False, flip(1), 5, side_y)

    total = part[mj].astype(F32)
    for k, copy in enumerate(part_copies):
        copy.wait_recv()
        total = total + part_in[k].astype(F32)
    residual = tok[mj].astype(F32) + total
    res[...] = residual
    hid[mj] = layer_norm(residual).astype(BF16)
    hid_copies = mlp_copies(lambda peer: hid.at[mj], lambda k: hid.at[mj], hid_s, hid_r)

    for copy in hid_copies:
        copy.wait_recv()

    rows_in = fg.shape[1]
    inner = fg.shape[2]
    tile = min(256, inner // 2)
    if n == 8:
        pair = 2 * rows_in

        def lanes(i):
            return pl.ds(pl.multiple_of(i // 2 * pair, pair), pair)

        def exchange(source, there, slot, peer):
            copy = pltpu.make_async_remote_copy(
                src_ref=source,
                dst_ref=there,
                send_sem=x_s.at[slot],
                recv_sem=x_r.at[slot],
                device_id={"req": peer},
                device_id_type=MESH,
            )
            copy.start()
            return copy

        near, far = pl.ds(0, pair), pl.ds(pair, pair)
        x_copies = [
            exchange(hid.at[:, :, lanes(flip(2))], hx.at[:, :, near], 0, flip(2)),
            exchange(hid.at[:, :, lanes(flip(6))], hx.at[:, :, far], 1, flip(2)),
            exchange(hid.at[:, :, lanes(flip(4))], hy.at[:, :, near], 2, flip(4)),
            exchange(hid.at[:, :, lanes(flip(6))], hy.at[:, :, far], 3, flip(4)),
        ]
        for slot in (2, 4, 5):
            arrived(slot)
        for copy in loads[7:]:
            copy.wait()

        def partial_sums(other, start, mate, theirs):
            @pl.loop(0, edge // tile)
            def _(c):
                cols = pl.ds(pl.multiple_of(start + c * tile, tile), tile)
                g = jnp.zeros((2 * rows, tile), F32)
                u = jnp.zeros((2 * rows, tile), F32)
                for place, base in ((near, me // 2), (far, mate // 2)):
                    a = jnp.concatenate(
                        [
                            hid[:, :, lanes(2 * base)].reshape(rows, pair),
                            other[:, :, place].reshape(rows, pair),
                        ],
                        axis=0,
                    )
                    for odd in range(2):
                        piece = a[:, odd * rows_in : (odd + 1) * rows_in]
                        g = g + mm(piece, fg[2 * base + odd, :, cols])
                        u = u + mm(piece, fu[2 * base + odd, :, cols])
                og[:, cols] = g[:rows]
                ou[:, cols] = u[:rows]
                here = pl.ds(pl.multiple_of(c * tile, tile), tile)
                theirs[0, :, here] = g[rows:].astype(BF16)
                theirs[1, :, here] = u[rows:].astype(BF16)

        x_copies[0].wait_recv()
        x_copies[1].wait_recv()
        partial_sums(hx, 0, flip(4), sx)
        x_copies.append(exchange(sx, rx, 4, flip(2)))
        x_copies[2].wait_recv()
        x_copies[3].wait_recv()
        partial_sums(hy, edge, flip(2), sy)
        x_copies.append(exchange(sy, ry, 5, flip(4)))
        send_states(flip(7), 6)
        arrived(3)
        send_shard(flip(6), False, flip(1), 6, ("d0", "d1"))
        for copy, got, start in ((x_copies[4], rx, 0), (x_copies[5], ry, edge)):
            copy.wait_recv()
            cols = pl.ds(start, edge)
            g = og[:, cols] + got[0].astype(F32)
            u = ou[:, cols] + got[1].astype(F32)
            hs[:, cols] = (g / (1.0 + jnp.exp(-g)) * u).astype(BF16)
        arrived(6)
    else:
        x_copies = []
        for slot in range(n - 1):
            arrived(slot)
        for copy in loads[7:]:
            copy.wait()

        @pl.loop(0, inner // tile)
        def _(c):
            cols = pl.ds(pl.multiple_of(c * tile, tile), tile)
            g = jnp.zeros((rows, tile), F32)
            u = jnp.zeros((rows, tile), F32)
            for i in range(n):
                a = hid[:, :, i * rows_in : (i + 1) * rows_in].reshape(rows, rows_in)
                g = g + mm(a, fg[i, :, cols])
                u = u + mm(a, fu[i, :, cols])
            hs[:, cols] = (g / (1.0 + jnp.exp(-g)) * u).astype(BF16)

    wide = fd.shape[2]

    @pl.loop(0, n)
    def _(i):
        cols = pl.ds(pl.multiple_of(i * wide, wide), wide)
        part2[:, :, cols] = mm(hs[...], fd[i]).astype(BF16).reshape(m, share, wide)

    part2_copies = mlp_copies(
        lambda peer: part2.at[peer], lambda k: part2_in.at[k - 1], part2_s, part2_r
    )
    total = part2[mj].astype(F32)
    for k, copy in enumerate(part2_copies):
        copy.wait_recv()
        total = total + part2_in[k].astype(F32)
    mixed[...] = (res[...] + total).astype(BF16)

    keep.wait()
    for copy in st_copies:
        copy.wait()
    for copy in tok_copies + part_copies + hid_copies + part2_copies + x_copies:
        copy.wait_send()
    for copy in w_copies.values():
        copy.wait_send()


def per_device(
    tokens,
    cached_states,
    prompt_lengths,
    accepted,
    owner_slot,
    w_query,
    w_key,
    w_value,
    w_gate_ret,
    w_out,
    w_gate,
    w_up,
    w_down,
):
    requests, heads, dk, dv = cached_states.shape
    n = lax.axis_size("req")
    m = lax.axis_size("mlp")
    share, width = tokens.shape
    rows = requests * DRAFT
    vmem = pl.BlockSpec(memory_space=pltpu.VMEM)
    smem = pl.BlockSpec(memory_space=pltpu.SMEM)
    hbm = pl.BlockSpec(memory_space=pl.ANY)
    dma = pltpu.SemaphoreType.DMA

    def v(shape, dtype=BF16):
        return pltpu.VMEM(shape, dtype)

    mixed, moved = pl.pallas_call(
        functools.partial(kernel, n, m),
        out_shape=(
            jax.ShapeDtypeStruct((share, width), BF16),
            jax.ShapeDtypeStruct((requests, heads, dk, dv), BF16),
        ),
        in_specs=[smem] * 3 + [hbm] * 10,
        out_specs=(vmem, hbm),
        scratch_shapes=[
            v(w_query.shape),
            v(w_key.shape),
            v(w_value.shape),
            v(w_gate_ret.shape),
            v(w_out.shape),
            v(cached_states.shape, F32),
            v((n,) + w_gate.shape),
            v((n,) + w_up.shape),
            v((n,) + w_down.shape),
            v((m, share, width)),
            v((rows, width)),
            v((rows, heads * dk)),
            v((requests, DRAFT, heads * dk)),
            v((requests, DRAFT, heads * dv)),
            v((rows, heads * dk)),
            v((rows, heads * dv), F32),
            v((rows, heads * dv), F32),
            v((rows, heads * dv)),
            v((m, share, width)),
            v((m - 1, share, width)),
            v((share, width), F32),
            v((m, share, width)),
            v((rows, w_gate.shape[1])),
            v((m, share, width)),
            v((m - 1, share, width)),
            v(cached_states.shape),
            v((m, share, 4 * w_gate.shape[0])),
            v((m, share, 4 * w_gate.shape[0])),
            v((2, rows, w_gate.shape[1] // 2)),
            v((2, rows, w_gate.shape[1] // 2)),
            v((2, rows, w_gate.shape[1] // 2)),
            v((2, rows, w_gate.shape[1] // 2)),
            v((rows, w_gate.shape[1]), F32),
            v((rows, w_gate.shape[1]), F32),
            dma((11,)),
            dma((m - 1,)),
            dma((m - 1,)),
            dma((m - 1,)),
            dma((m - 1,)),
            dma((m - 1,)),
            dma((m - 1,)),
            dma((m - 1,)),
            dma((m - 1,)),
            dma((n - 1, 4)),
            dma((n - 1, 4)),
            dma((n - 1,)),
            dma((n - 1,)),
            dma((6,)),
            dma((6,)),
        ],
        compiler_params=pltpu.CompilerParams(
            collective_id=0, has_side_effects=True, vmem_limit_bytes=60 * 1024 * 1024
        ),
    )(
        prompt_lengths,
        accepted,
        owner_slot,
        tokens,
        cached_states,
        w_query,
        w_key,
        w_value,
        w_gate_ret,
        w_out,
        w_gate,
        w_up,
        w_down,
    )
    return (mixed, moved.astype(F32))


def solution(mesh):
    return jax.shard_map(
        per_device,
        mesh=mesh,
        in_specs=(
            P(("req", "mlp"), None),
            P("req", "mlp", None, None),
            P("req"),
            P("req"),
            P("req"),
            P(None, "mlp"),
            P(None, "mlp"),
            P(None, "mlp"),
            P(None, "mlp"),
            P("mlp", None),
            P("req", "mlp"),
            P("req", "mlp"),
            P("mlp", "req"),
        ),
        out_specs=(P(("req", "mlp"), None), P("req", "mlp", None, None)),
        check_vma=False,
    )
```

```python
import functools
import math

import jax
import jax.numpy as jnp
from jax import lax
from jax.experimental import pallas as pl
from jax.experimental.pallas import tpu as pltpu
from jax.sharding import PartitionSpec as P

DRAFT = 16


epsilon = 1e-05


def layer_norm(inputs):
    average = jnp.mean(inputs, axis=-1, keepdims=True)
    centred = inputs - average
    variance = jnp.mean(centred * centred, axis=-1, keepdims=True)
    return centred * lax.rsqrt(variance + epsilon)


MESH = pl.DeviceIdType.MESH
F32 = jnp.float32
BF16 = jnp.bfloat16


def mm(a, b):
    return jnp.dot(a, b, preferred_element_type=F32)


def kernel(
    n,
    m,
    prompt,
    accepted,
    slots,
    tokens,
    states,
    w_query,
    w_key,
    w_value,
    w_gate_ret,
    w_out,
    w_gate,
    w_up,
    w_down,
    mixed,
    moved,
    wq,
    wk,
    wv,
    wgr,
    wo,
    st,
    fg,
    fu,
    fd,
    tok,
    normed,
    rq,
    ksc,
    vals,
    rk_h,
    gated,
    outs,
    joined,
    part,
    part_in,
    res,
    hid,
    hs,
    part2,
    part2_in,
    send_buf,
    hx,
    hy,
    sx,
    sy,
    rx,
    ry,
    og,
    ou,
    load_sem,
    tok_s,
    tok_r,
    part_s,
    part_r,
    hid_s,
    hid_r,
    part2_s,
    part2_r,
    w_s,
    w_r,
    st_s,
    st_r,
    x_s,
    x_r,
):
    me = lax.axis_index("req")
    mj = lax.axis_index("mlp")
    share, width = tokens.shape
    requests, heads, dk, dv = states.shape
    rows = m * share
    half = dk // 2
    per_peer = requests // n
    draft = DRAFT

    barrier = pltpu.get_barrier_semaphore()
    for k in range(1, n):
        pl.semaphore_signal(
            barrier, inc=1, device_id={"req": lax.rem(me + k, n)}, device_id_type=MESH
        )
    for k in range(1, m):
        pl.semaphore_signal(
            barrier, inc=1, device_id={"mlp": lax.rem(mj + k, m)}, device_id_type=MESH
        )

    loads = []
    for a, b in (
        (tokens, tok.at[mj]),
        (w_query, wq),
        (w_key, wk),
        (w_value, wv),
        (w_gate_ret, wgr),
        (states, st),
        (w_out, wo),
        (w_gate, fg.at[me]),
        (w_up, fu.at[me]),
        (w_down, fd.at[me]),
    ):
        copy = pltpu.make_async_copy(a, b, load_sem.at[len(loads)])
        copy.start()
        loads.append(copy)

    pl.semaphore_wait(barrier, n + m - 2)

    def mlp_copies(pick, dst, s, r, base=0):
        copies = []
        for k in range(1, m):
            peer = lax.rem(mj + k, m)
            copies.append(
                pltpu.make_async_remote_copy(
                    src_ref=pick(peer),
                    dst_ref=dst(k),
                    send_sem=s.at[base + k - 1],
                    recv_sem=r.at[base + k - 1],
                    device_id={"mlp": peer},
                    device_id_type=MESH,
                )
            )
        for copy in copies:
            copy.start()
        return copies

    tok_copies = mlp_copies(lambda peer: tokens, lambda k: tok.at[mj], tok_s, tok_r)

    cut = w_down.shape[0] // 2
    edge = w_gate.shape[1] // 2
    both = pl.ds(0, w_gate.shape[0])
    cut_of = {
        "g": (w_gate, fg, ()),
        "u": (w_up, fu, ()),
        "ga": (w_gate, fg, (both, pl.ds(0, edge))),
        "gb": (w_gate, fg, (both, pl.ds(edge, edge))),
        "ua": (w_up, fu, (both, pl.ds(0, edge))),
        "ub": (w_up, fu, (both, pl.ds(edge, edge))),
        "d0": (w_down, fd, (pl.ds(0, cut),)),
        "d1": (w_down, fd, (pl.ds(cut, cut),)),
    }

    w_copies = {}

    def send_shard(owner, own, peer, slot, names=("g", "u", "d0", "d1"), at=0):
        for i, name in enumerate(names):
            given, held, where = cut_of[name]
            there = held.at[(owner,) + where]
            copy = pltpu.make_async_remote_copy(
                src_ref=(given.at[where] if where else given) if own else there,
                dst_ref=there,
                send_sem=w_s.at[slot, at + i],
                recv_sem=w_r.at[slot, at + i],
                device_id={"req": peer},
                device_id_type=MESH,
            )
            copy.start()
            w_copies[slot, at + i] = copy

    def arrived(slot):
        for (at, _), copy in w_copies.items():
            if at == slot:
                copy.wait_recv()

    def flip(bits):
        out = me
        for bit in (1, 2, 4):
            if bits & bit:
                out = out + bit - 2 * bit * lax.rem(out // bit, 2)
        return out

    if n == 8:
        side_x = ("gb", "ub", "d0", "d1")
        side_y = ("ga", "ua", "d0", "d1")
        send_shard(me, True, flip(2), 0, side_x)
        send_shard(me, True, flip(4), 1, side_y)
        send_shard(me, True, flip(1), 2)
    else:
        for k in range(1, n):
            send_shard(me, True, lax.rem(me + k, n), k - 1)

    row = lax.broadcasted_iota(jnp.int32, (rows, half), 0)
    draft_pos = lax.rem(row, draft)
    start = jnp.zeros((rows, half), jnp.int32)
    kept = jnp.zeros((rows, half), jnp.int32)
    for r in range(requests):
        start = jnp.where(row >= r * draft, prompt[r], start)
        kept = jnp.where(row >= r * draft, accepted[r], kept)
    lane = lax.broadcasted_iota(jnp.int32, (rows, half), 1).astype(F32)
    angles = (start + draft_pos).astype(F32) * jnp.exp(-math.log(10000.0) * lane / half)
    cos_part, sin_part = jnp.cos(angles), jnp.sin(angles)
    exponent = (kept - 1 - draft_pos).astype(F32)
    to = lax.broadcasted_iota(jnp.int32, (rows, rows), 0)
    source = lax.broadcasted_iota(jnp.int32, (rows, rows), 1)
    causal = (to // draft == source // draft) & (to >= source)
    distance = (to - source).astype(F32)

    def log_gamma(h, shape):
        head = jnp.full(shape, mj * heads + h, jnp.int32).astype(F32)
        return jnp.log(1.0 - jnp.exp2(-5.0 - head))

    fold, mask, carry = [], [], []
    for h in range(heads):
        lg = log_gamma(h, (1, half))
        weight = jnp.where(exponent >= 0, jnp.exp(jnp.maximum(exponent, 0.0) * lg), 0.0)
        fold.append(jnp.concatenate([weight, weight], axis=-1))
        carry.append(jnp.exp((draft_pos.astype(F32) + 1.0) * lg)[:, :1])
        mask.append(
            jnp.where(
                causal, jnp.exp(jnp.maximum(distance, 0.0) * log_gamma(h, (1, rows))), 0.0
            )
        )

    loads[0].wait()
    for copy in tok_copies:
        copy.wait_recv()
    normed[...] = layer_norm(tok[...].astype(F32).reshape(rows, width)).astype(BF16)

    def turned(v):
        front, back = v[:, :half], v[:, half:]
        return jnp.concatenate(
            [front * cos_part - back * sin_part, front * sin_part + back * cos_part], axis=-1
        ).astype(BF16)

    loads[1].wait()
    loads[2].wait()
    for h in range(heads):
        cols = pl.ds(h * dk, dk)
        rq[:, cols] = turned(mm(normed[...], wq[:, cols]))
        rk = turned(mm(normed[...], wk[:, cols]) * (1.0 / math.sqrt(dk)))
        rk_h[:, cols] = rk
        ksc[:, :, cols] = (
            (rk.astype(F32) * fold[h]).astype(BF16).reshape(requests, draft, dk)
        )
    loads[3].wait()
    for h in range(heads):
        cols = pl.ds(h * dv, dv)
        vals[:, :, cols] = mm(normed[...], wv[:, cols]).astype(BF16).reshape(
            requests, draft, dv
        )
    loads[5].wait()

    st_copies = []

    def fresh(p):
        r = 0
        for q in range(requests):
            slot = slots[q]
            place = slot // requests * per_peer + lax.rem(slot, per_peer)
            r = jnp.where(place == p, q, r)
        count = jnp.full((1, dv), accepted[r], jnp.int32).astype(F32)
        for h in range(heads):
            old_scale = jnp.exp(count * log_gamma(h, (1, dv)))
            update = lax.dot_general(
                ksc[r, :, h * dk : (h + 1) * dk],
                vals[r, :, h * dv : (h + 1) * dv],
                (((0,), (0,)), ((), ())),
                preferred_element_type=F32,
            )
            send_buf[p, h] = (old_scale * st[r, h] + update).astype(BF16)

    pl.loop(0, requests)(fresh)
    mine = pl.ds(me * per_peer, per_peer)

    def send_states(peer, slot):
        copy = pltpu.make_async_remote_copy(
            src_ref=send_buf.at[pl.ds(peer * per_peer, per_peer)],
            dst_ref=moved.at[mine],
            send_sem=st_s.at[slot],
            recv_sem=st_r.at[slot],
            device_id={"req": peer},
            device_id_type=MESH,
        )
        copy.start()
        st_copies.append(copy)

    if n == 8:
        for bits in (2, 4, 6, 3, 5, 1):
            send_states(flip(bits), bits - 1)
    else:
        for k in range(1, n):
            send_states(lax.rem(me + k, n), k - 1)
    keep = pltpu.make_async_copy(send_buf.at[mine], moved.at[mine], load_sem.at[10])
    keep.start()

    loads[4].wait()
    for h in range(heads):
        cols = pl.ds(h * dv, dv)
        g = mm(normed[...], wgr[:, cols])
        gated[:, cols] = g / (1.0 + jnp.exp(-g))

    @pl.loop(0, requests)
    def _(r):
        here = pl.ds(pl.multiple_of(r * draft, draft), draft)
        for h in range(heads):
            outs[here, h * dv : (h + 1) * dv] = mm(
                rq[here, h * dk : (h + 1) * dk], st[r, h].astype(BF16)
            )

    for h in range(heads):
        cols = pl.ds(h * dk, dk)
        vcols = pl.ds(h * dv, dv)
        scores = lax.dot_general(
            rq[:, cols], rk_h[:, cols], (((1,), (1,)), ((), ())), preferred_element_type=F32
        )
        weights = (scores * mask[h]).astype(BF16)
        out = mm(weights, vals[:, :, vcols].reshape(rows, dv)) + outs[:, vcols] * carry[h]
        joined[:, vcols] = (layer_norm(out) * gated[:, vcols]).astype(BF16)

    loads[6].wait()
    step = min(512, width // 2)

    middle = width // 2
    part_copies = []
    for side in range(2):

        @pl.loop(0, middle // step)
        def _(c):
            cols = pl.ds(pl.multiple_of(side * middle + c * step, step), step)
            part[:, :, cols] = (
                mm(joined[...], wo[:, cols]).astype(BF16).reshape(m, share, step)
            )

        span = pl.ds(side * middle, middle)
        part_copies += mlp_copies(
            lambda peer: part.at[peer, :, span],
            lambda k: part_in.at[k - 1, :, span],
            part_s,
            part_r,
            side * (m - 1),
        )

    if n == 8:
        arrived(0)
        send_shard(flip(2), False, flip(4), 3, ("d0",))
        arrived(1)
        send_shard(flip(4), False, flip(2), 3, ("d1",), 1)
        send_shard(flip(2), False, flip(1), 4, side_x)
        send_shard(flip(4), False, flip(1), 5, side_y)

    total = part[mj].astype(F32)
    for copy in part_copies:
        copy.wait_recv()
    for k in range(m - 1):
        total = total + part_in[k].astype(F32)
    residual = tok[mj].astype(F32) + total
    res[...] = residual
    hid[mj] = layer_norm(residual).astype(BF16)
    hid_copies = mlp_copies(lambda peer: hid.at[mj], lambda k: hid.at[mj], hid_s, hid_r)

    rows_in = fg.shape[1]
    inner = fg.shape[2]
    tile = min(256, inner // 2)
    if n == 8:
        pair = 2 * rows_in

        def lanes(i):
            return pl.ds(pl.multiple_of(i // 2 * pair, pair), pair)

        def exchange(source, there, slot, peer):
            copy = pltpu.make_async_remote_copy(
                src_ref=source,
                dst_ref=there,
                send_sem=x_s.at[slot],
                recv_sem=x_r.at[slot],
                device_id={"req": peer},
                device_id_type=MESH,
            )
            copy.start()
            return copy

        near, far = pl.ds(0, pair), pl.ds(pair, pair)
        to_x, to_y = [], []
        for k in range(m):
            if k > 0:
                hid_copies[k - 1].wait_recv()
            came = lax.rem(mj + m - k, m)
            at = 2 + 4 * k
            chunk = hid.at[came]
            to_x += [
                exchange(chunk.at[:, lanes(flip(2))], hx.at[came, :, near], at, flip(2)),
                exchange(chunk.at[:, lanes(flip(6))], hx.at[came, :, far], at + 1, flip(2)),
            ]
            to_y += [
                exchange(chunk.at[:, lanes(flip(4))], hy.at[came, :, near], at + 2, flip(4)),
                exchange(chunk.at[:, lanes(flip(6))], hy.at[came, :, far], at + 3, flip(4)),
            ]
        for slot in (2, 4, 5):
            arrived(slot)
        for copy in loads[7:]:
            copy.wait()

        def partial_sums(other, start, mate, theirs):
            @pl.loop(0, edge // tile)
            def _(c):
                cols = pl.ds(pl.multiple_of(start + c * tile, tile), tile)
                g = jnp.zeros((2 * rows, tile), F32)
                u = jnp.zeros((2 * rows, tile), F32)
                for place, base in ((near, me // 2), (far, mate // 2)):
                    a = jnp.concatenate(
                        [
                            hid[:, :, lanes(2 * base)].reshape(rows, pair),
                            other[:, :, place].reshape(rows, pair),
                        ],
                        axis=0,
                    )
                    for odd in range(2):
                        piece = a[:, odd * rows_in : (odd + 1) * rows_in]
                        g = g + mm(piece, fg[2 * base + odd, :, cols])
                        u = u + mm(piece, fu[2 * base + odd, :, cols])
                og[:, cols] = g[:rows]
                ou[:, cols] = u[:rows]
                here = pl.ds(pl.multiple_of(c * tile, tile), tile)
                theirs[0, :, here] = g[rows:].astype(BF16)
                theirs[1, :, here] = u[rows:].astype(BF16)

        for copy in to_x:
            copy.wait_recv()
        partial_sums(hx, 0, flip(4), sx)
        sum_x = exchange(sx, rx, 0, flip(2))
        for copy in to_y:
            copy.wait_recv()
        partial_sums(hy, edge, flip(2), sy)
        sum_y = exchange(sy, ry, 1, flip(4))
        x_copies = to_x + to_y + [sum_x, sum_y]
        send_states(flip(7), 6)
        arrived(3)
        send_shard(flip(6), False, flip(1), 6, ("d0", "d1"))
        for copy, got, start in ((sum_x, rx, 0), (sum_y, ry, edge)):
            copy.wait_recv()
            cols = pl.ds(start, edge)
            g = og[:, cols] + got[0].astype(F32)
            u = ou[:, cols] + got[1].astype(F32)
            hs[:, cols] = (g / (1.0 + jnp.exp(-g)) * u).astype(BF16)
        arrived(6)
    else:
        x_copies = []
        for copy in hid_copies:
            copy.wait_recv()
        for slot in range(n - 1):
            arrived(slot)
        for copy in loads[7:]:
            copy.wait()

        @pl.loop(0, inner // tile)
        def _(c):
            cols = pl.ds(pl.multiple_of(c * tile, tile), tile)
            g = jnp.zeros((rows, tile), F32)
            u = jnp.zeros((rows, tile), F32)
            for i in range(n):
                a = hid[:, :, i * rows_in : (i + 1) * rows_in].reshape(rows, rows_in)
                g = g + mm(a, fg[i, :, cols])
                u = u + mm(a, fu[i, :, cols])
            hs[:, cols] = (g / (1.0 + jnp.exp(-g)) * u).astype(BF16)

    wide = fd.shape[2]

    part2_copies = []
    for side in range(2):

        @pl.loop(side * n // 2, (side + 1) * n // 2)
        def _(i):
            cols = pl.ds(pl.multiple_of(i * wide, wide), wide)
            part2[:, :, cols] = mm(hs[...], fd[i]).astype(BF16).reshape(m, share, wide)

        span = pl.ds(side * middle, middle)
        part2_copies += mlp_copies(
            lambda peer: part2.at[peer, :, span],
            lambda k: part2_in.at[k - 1, :, span],
            part2_s,
            part2_r,
            side * (m - 1),
        )
    total = part2[mj].astype(F32)
    for copy in part2_copies:
        copy.wait_recv()
    for k in range(m - 1):
        total = total + part2_in[k].astype(F32)
    mixed[...] = (res[...] + total).astype(BF16)

    keep.wait()
    for copy in st_copies:
        copy.wait()
    for copy in tok_copies + part_copies + hid_copies + part2_copies + x_copies:
        copy.wait_send()
    for copy in w_copies.values():
        copy.wait_send()


def per_device(
    tokens,
    cached_states,
    prompt_lengths,
    accepted,
    owner_slot,
    w_query,
    w_key,
    w_value,
    w_gate_ret,
    w_out,
    w_gate,
    w_up,
    w_down,
):
    requests, heads, dk, dv = cached_states.shape
    n = lax.axis_size("req")
    m = lax.axis_size("mlp")
    share, width = tokens.shape
    rows = requests * DRAFT
    vmem = pl.BlockSpec(memory_space=pltpu.VMEM)
    smem = pl.BlockSpec(memory_space=pltpu.SMEM)
    hbm = pl.BlockSpec(memory_space=pl.ANY)
    dma = pltpu.SemaphoreType.DMA

    def v(shape, dtype=BF16):
        return pltpu.VMEM(shape, dtype)

    mixed, moved = pl.pallas_call(
        functools.partial(kernel, n, m),
        out_shape=(
            jax.ShapeDtypeStruct((share, width), BF16),
            jax.ShapeDtypeStruct((requests, heads, dk, dv), BF16),
        ),
        in_specs=[smem] * 3 + [hbm] * 10,
        out_specs=(vmem, hbm),
        scratch_shapes=[
            v(w_query.shape),
            v(w_key.shape),
            v(w_value.shape),
            v(w_gate_ret.shape),
            v(w_out.shape),
            v(cached_states.shape, F32),
            v((n,) + w_gate.shape),
            v((n,) + w_up.shape),
            v((n,) + w_down.shape),
            v((m, share, width)),
            v((rows, width)),
            v((rows, heads * dk)),
            v((requests, DRAFT, heads * dk)),
            v((requests, DRAFT, heads * dv)),
            v((rows, heads * dk)),
            v((rows, heads * dv), F32),
            v((rows, heads * dv), F32),
            v((rows, heads * dv)),
            v((m, share, width)),
            v((m - 1, share, width)),
            v((share, width), F32),
            v((m, share, width)),
            v((rows, w_gate.shape[1])),
            v((m, share, width)),
            v((m - 1, share, width)),
            v(cached_states.shape),
            v((m, share, 4 * w_gate.shape[0])),
            v((m, share, 4 * w_gate.shape[0])),
            v((2, rows, w_gate.shape[1] // 2)),
            v((2, rows, w_gate.shape[1] // 2)),
            v((2, rows, w_gate.shape[1] // 2)),
            v((2, rows, w_gate.shape[1] // 2)),
            v((rows, w_gate.shape[1]), F32),
            v((rows, w_gate.shape[1]), F32),
            dma((11,)),
            dma((m - 1,)),
            dma((m - 1,)),
            dma((2 * (m - 1),)),
            dma((2 * (m - 1),)),
            dma((m - 1,)),
            dma((m - 1,)),
            dma((2 * (m - 1),)),
            dma((2 * (m - 1),)),
            dma((n - 1, 4)),
            dma((n - 1, 4)),
            dma((n - 1,)),
            dma((n - 1,)),
            dma((2 + 4 * m,)),
            dma((2 + 4 * m,)),
        ],
        compiler_params=pltpu.CompilerParams(
            collective_id=0, has_side_effects=True, vmem_limit_bytes=60 * 1024 * 1024
        ),
    )(
        prompt_lengths,
        accepted,
        owner_slot,
        tokens,
        cached_states,
        w_query,
        w_key,
        w_value,
        w_gate_ret,
        w_out,
        w_gate,
        w_up,
        w_down,
    )
    return (mixed, moved.astype(F32))


def solution(mesh):
    return jax.shard_map(
        per_device,
        mesh=mesh,
        in_specs=(
            P(("req", "mlp"), None),
            P("req", "mlp", None, None),
            P("req"),
            P("req"),
            P("req"),
            P(None, "mlp"),
            P(None, "mlp"),
            P(None, "mlp"),
            P(None, "mlp"),
            P("mlp", None),
            P("req", "mlp"),
            P("req", "mlp"),
            P("mlp", "req"),
        ),
        out_specs=(P(("req", "mlp"), None), P("req", "mlp", None, None)),
        check_vma=False,
    )
```

```python
import functools
import math

import jax
import jax.numpy as jnp
from jax import lax
from jax.experimental import pallas as pl
from jax.experimental.pallas import tpu as pltpu
from jax.sharding import PartitionSpec as P

DRAFT = 16


epsilon = 1e-05


def layer_norm(inputs):
    average = jnp.mean(inputs, axis=-1, keepdims=True)
    centred = inputs - average
    variance = jnp.mean(centred * centred, axis=-1, keepdims=True)
    return centred * lax.rsqrt(variance + epsilon)


MESH = pl.DeviceIdType.MESH
F32 = jnp.float32
BF16 = jnp.bfloat16


def mm(a, b):
    return jnp.dot(a, b, preferred_element_type=F32)


def kernel(
    n,
    m,
    prompt,
    accepted,
    slots,
    tokens,
    states,
    w_query,
    w_key,
    w_value,
    w_gate_ret,
    w_out,
    w_gate,
    w_up,
    w_down,
    mixed,
    moved,
    wq,
    wk,
    wv,
    wgr,
    wo,
    st,
    fg,
    fu,
    fd,
    tok,
    normed,
    rq,
    ksc,
    vals,
    rk_h,
    gated,
    outs,
    joined,
    part,
    part_in,
    res,
    hid,
    hs,
    part2,
    part2_in,
    send_buf,
    hx,
    hy,
    sx,
    sy,
    rx,
    ry,
    og,
    ou,
    load_sem,
    tok_s,
    tok_r,
    part_s,
    part_r,
    hid_s,
    hid_r,
    part2_s,
    part2_r,
    w_s,
    w_r,
    st_s,
    st_r,
    x_s,
    x_r,
):
    me = lax.axis_index("req")
    mj = lax.axis_index("mlp")
    share, width = tokens.shape
    requests, heads, dk, dv = states.shape
    rows = m * share
    half = dk // 2
    per_peer = requests // n
    draft = DRAFT

    barrier = pltpu.get_barrier_semaphore()
    for k in range(1, n):
        pl.semaphore_signal(
            barrier, inc=1, device_id={"req": lax.rem(me + k, n)}, device_id_type=MESH
        )
    for k in range(1, m):
        pl.semaphore_signal(
            barrier, inc=1, device_id={"mlp": lax.rem(mj + k, m)}, device_id_type=MESH
        )

    loads = []
    for a, b in (
        (tokens, tok.at[mj]),
        (w_query, wq),
        (w_key, wk),
        (w_value, wv),
        (w_gate_ret, wgr),
        (states, st),
        (w_out, wo),
        (w_gate, fg.at[me]),
        (w_up, fu.at[me]),
        (w_down, fd.at[me]),
    ):
        copy = pltpu.make_async_copy(a, b, load_sem.at[len(loads)])
        copy.start()
        loads.append(copy)

    pl.semaphore_wait(barrier, n + m - 2)

    def mlp_copies(pick, dst, s, r, base=0):
        copies = []
        for k in range(1, m):
            peer = lax.rem(mj + k, m)
            copies.append(
                pltpu.make_async_remote_copy(
                    src_ref=pick(peer),
                    dst_ref=dst(k),
                    send_sem=s.at[base + k - 1],
                    recv_sem=r.at[base + k - 1],
                    device_id={"mlp": peer},
                    device_id_type=MESH,
                )
            )
        for copy in copies:
            copy.start()
        return copies

    tok_copies = mlp_copies(lambda peer: tokens, lambda k: tok.at[mj], tok_s, tok_r)

    cut = w_down.shape[0] // 2
    edge = w_gate.shape[1] // 2
    both = pl.ds(0, w_gate.shape[0])
    cut_of = {
        "g": (w_gate, fg, ()),
        "u": (w_up, fu, ()),
        "ga": (w_gate, fg, (both, pl.ds(0, edge))),
        "gb": (w_gate, fg, (both, pl.ds(edge, edge))),
        "ua": (w_up, fu, (both, pl.ds(0, edge))),
        "ub": (w_up, fu, (both, pl.ds(edge, edge))),
        "d0": (w_down, fd, (pl.ds(0, cut),)),
        "d1": (w_down, fd, (pl.ds(cut, cut),)),
    }

    w_copies = {}

    def send_shard(owner, own, peer, slot, names=("g", "u", "d0", "d1"), at=0):
        for i, name in enumerate(names):
            given, held, where = cut_of[name]
            there = held.at[(owner,) + where]
            copy = pltpu.make_async_remote_copy(
                src_ref=(given.at[where] if where else given) if own else there,
                dst_ref=there,
                send_sem=w_s.at[slot, at + i],
                recv_sem=w_r.at[slot, at + i],
                device_id={"req": peer},
                device_id_type=MESH,
            )
            copy.start()
            w_copies[slot, at + i] = copy

    def arrived(slot):
        for (at, _), copy in w_copies.items():
            if at == slot:
                copy.wait_recv()

    def flip(bits):
        out = me
        for bit in (1, 2, 4):
            if bits & bit:
                out = out + bit - 2 * bit * lax.rem(out // bit, 2)
        return out

    if n == 8:
        side_x = ("gb", "ub", "d0", "d1")
        side_y = ("ga", "ua", "d0", "d1")
        send_shard(me, True, flip(2), 0, side_x)
        send_shard(me, True, flip(4), 1, side_y)
        send_shard(me, True, flip(1), 2)
    else:
        for k in range(1, n):
            send_shard(me, True, lax.rem(me + k, n), k - 1)

    row = lax.broadcasted_iota(jnp.int32, (rows, half), 0)
    draft_pos = lax.rem(row, draft)
    start = jnp.zeros((rows, half), jnp.int32)
    kept = jnp.zeros((rows, half), jnp.int32)
    for r in range(requests):
        start = jnp.where(row >= r * draft, prompt[r], start)
        kept = jnp.where(row >= r * draft, accepted[r], kept)
    lane = lax.broadcasted_iota(jnp.int32, (rows, half), 1).astype(F32)
    angles = (start + draft_pos).astype(F32) * jnp.exp(-math.log(10000.0) * lane / half)
    cos_part, sin_part = jnp.cos(angles), jnp.sin(angles)
    exponent = (kept - 1 - draft_pos).astype(F32)
    to = lax.broadcasted_iota(jnp.int32, (rows, rows), 0)
    source = lax.broadcasted_iota(jnp.int32, (rows, rows), 1)
    causal = (to // draft == source // draft) & (to >= source)
    distance = (to - source).astype(F32)

    def log_gamma(h, shape):
        head = jnp.full(shape, mj * heads + h, jnp.int32).astype(F32)
        return jnp.log(1.0 - jnp.exp2(-5.0 - head))

    fold, mask, carry = [], [], []
    for h in range(heads):
        lg = log_gamma(h, (1, half))
        weight = jnp.where(exponent >= 0, jnp.exp(jnp.maximum(exponent, 0.0) * lg), 0.0)
        fold.append(jnp.concatenate([weight, weight], axis=-1))
        carry.append(jnp.exp((draft_pos.astype(F32) + 1.0) * lg)[:, :1])
        mask.append(
            jnp.where(
                causal, jnp.exp(jnp.maximum(distance, 0.0) * log_gamma(h, (1, rows))), 0.0
            )
        )

    loads[0].wait()
    for copy in tok_copies:
        copy.wait_recv()
    normed[...] = layer_norm(tok[...].astype(F32).reshape(rows, width)).astype(BF16)

    def turned(v):
        front, back = v[:, :half], v[:, half:]
        return jnp.concatenate(
            [front * cos_part - back * sin_part, front * sin_part + back * cos_part], axis=-1
        ).astype(BF16)

    loads[1].wait()
    loads[2].wait()
    for h in range(heads):
        cols = pl.ds(h * dk, dk)
        rq[:, cols] = turned(mm(normed[...], wq[:, cols]))
        rk = turned(mm(normed[...], wk[:, cols]) * (1.0 / math.sqrt(dk)))
        rk_h[:, cols] = rk
        ksc[:, :, cols] = (
            (rk.astype(F32) * fold[h]).astype(BF16).reshape(requests, draft, dk)
        )
    loads[3].wait()
    for h in range(heads):
        cols = pl.ds(h * dv, dv)
        vals[:, :, cols] = mm(normed[...], wv[:, cols]).astype(BF16).reshape(
            requests, draft, dv
        )
    loads[5].wait()

    st_copies = []

    def fresh(p):
        r = 0
        for q in range(requests):
            slot = slots[q]
            place = slot // requests * per_peer + lax.rem(slot, per_peer)
            r = jnp.where(place == p, q, r)
        count = jnp.full((1, dv), accepted[r], jnp.int32).astype(F32)
        for h in range(heads):
            old_scale = jnp.exp(count * log_gamma(h, (1, dv)))
            update = lax.dot_general(
                ksc[r, :, h * dk : (h + 1) * dk],
                vals[r, :, h * dv : (h + 1) * dv],
                (((0,), (0,)), ((), ())),
                preferred_element_type=F32,
            )
            send_buf[p, h] = (old_scale * st[r, h] + update).astype(BF16)

    pl.loop(0, requests)(fresh)
    mine = pl.ds(me * per_peer, per_peer)

    def send_states(peer, slot):
        copy = pltpu.make_async_remote_copy(
            src_ref=send_buf.at[pl.ds(peer * per_peer, per_peer)],
            dst_ref=moved.at[mine],
            send_sem=st_s.at[slot],
            recv_sem=st_r.at[slot],
            device_id={"req": peer},
            device_id_type=MESH,
        )
        copy.start()
        st_copies.append(copy)

    if n == 8:
        for bits in (2, 4, 6, 3, 5, 1):
            send_states(flip(bits), bits - 1)
    else:
        for k in range(1, n):
            send_states(lax.rem(me + k, n), k - 1)
    keep = pltpu.make_async_copy(send_buf.at[mine], moved.at[mine], load_sem.at[10])
    keep.start()

    loads[4].wait()
    for h in range(heads):
        cols = pl.ds(h * dv, dv)
        g = mm(normed[...], wgr[:, cols])
        gated[:, cols] = g / (1.0 + jnp.exp(-g))

    @pl.loop(0, requests)
    def _(r):
        here = pl.ds(pl.multiple_of(r * draft, draft), draft)
        for h in range(heads):
            outs[here, h * dv : (h + 1) * dv] = mm(
                rq[here, h * dk : (h + 1) * dk], st[r, h].astype(BF16)
            )

    for h in range(heads):
        cols = pl.ds(h * dk, dk)
        vcols = pl.ds(h * dv, dv)
        scores = lax.dot_general(
            rq[:, cols], rk_h[:, cols], (((1,), (1,)), ((), ())), preferred_element_type=F32
        )
        weights = (scores * mask[h]).astype(BF16)
        out = mm(weights, vals[:, :, vcols].reshape(rows, dv)) + outs[:, vcols] * carry[h]
        joined[:, vcols] = (layer_norm(out) * gated[:, vcols]).astype(BF16)

    loads[6].wait()
    step = min(512, width // 2)

    middle = width // 2
    part_copies = []
    for side in range(2):

        @pl.loop(0, middle // step)
        def _(c):
            cols = pl.ds(pl.multiple_of(side * middle + c * step, step), step)
            part[:, :, cols] = (
                mm(joined[...], wo[:, cols]).astype(BF16).reshape(m, share, step)
            )

        span = pl.ds(side * middle, middle)
        part_copies += mlp_copies(
            lambda peer: part.at[peer, :, span],
            lambda k: part_in.at[k - 1, :, span],
            part_s,
            part_r,
            side * (m - 1),
        )

    if n == 8:
        arrived(0)
        send_shard(flip(2), False, flip(4), 3, ("d0",))
        arrived(1)
        send_shard(flip(4), False, flip(2), 3, ("d1",), 1)
        send_shard(flip(2), False, flip(1), 4, side_x)
        send_shard(flip(4), False, flip(1), 5, side_y)

    total = part[mj].astype(F32)
    for copy in part_copies:
        copy.wait_recv()
    for k in range(m - 1):
        total = total + part_in[k].astype(F32)
    residual = tok[mj].astype(F32) + total
    res[...] = residual
    hid[mj] = layer_norm(residual).astype(BF16)
    hid_copies = mlp_copies(lambda peer: hid.at[mj], lambda k: hid.at[mj], hid_s, hid_r)

    rows_in = fg.shape[1]
    inner = fg.shape[2]
    tile = min(256, inner // 2)
    if n == 8:
        pair = 2 * rows_in

        def lanes(i):
            return pl.ds(pl.multiple_of(i // 2 * pair, pair), pair)

        def exchange(source, there, slot, peer):
            copy = pltpu.make_async_remote_copy(
                src_ref=source,
                dst_ref=there,
                send_sem=x_s.at[slot],
                recv_sem=x_r.at[slot],
                device_id={"req": peer},
                device_id_type=MESH,
            )
            copy.start()
            return copy

        near, far = pl.ds(0, pair), pl.ds(pair, pair)
        to_x, to_y = [], []
        for k in range(m):
            if k > 0:
                hid_copies[k - 1].wait_recv()
            came = lax.rem(mj + m - k, m)
            at = 2 + 4 * k
            chunk = hid.at[came]
            to_x += [
                exchange(chunk.at[:, lanes(flip(2))], hx.at[came, :, near], at, flip(2)),
                exchange(chunk.at[:, lanes(flip(6))], hx.at[came, :, far], at + 1, flip(2)),
            ]
            to_y += [
                exchange(chunk.at[:, lanes(flip(4))], hy.at[came, :, near], at + 2, flip(4)),
                exchange(chunk.at[:, lanes(flip(6))], hy.at[came, :, far], at + 3, flip(4)),
            ]
        send_states(flip(7), 6)
        for slot in (2, 4, 5):
            arrived(slot)
        for copy in loads[7:]:
            copy.wait()

        def partial_sums(other, start, mate, theirs):
            @pl.loop(0, edge // tile)
            def _(c):
                cols = pl.ds(pl.multiple_of(start + c * tile, tile), tile)
                g = jnp.zeros((2 * rows, tile), F32)
                u = jnp.zeros((2 * rows, tile), F32)
                for place, base in ((near, me // 2), (far, mate // 2)):
                    a = jnp.concatenate(
                        [
                            hid[:, :, lanes(2 * base)].reshape(rows, pair),
                            other[:, :, place].reshape(rows, pair),
                        ],
                        axis=0,
                    )
                    for odd in range(2):
                        piece = a[:, odd * rows_in : (odd + 1) * rows_in]
                        g = g + mm(piece, fg[2 * base + odd, :, cols])
                        u = u + mm(piece, fu[2 * base + odd, :, cols])
                og[:, cols] = g[:rows]
                ou[:, cols] = u[:rows]
                here = pl.ds(pl.multiple_of(c * tile, tile), tile)
                theirs[0, :, here] = g[rows:].astype(BF16)
                theirs[1, :, here] = u[rows:].astype(BF16)

        for copy in to_x:
            copy.wait_recv()
        partial_sums(hx, 0, flip(4), sx)
        sum_x = exchange(sx, rx, 0, flip(2))
        for copy in to_y:
            copy.wait_recv()
        partial_sums(hy, edge, flip(2), sy)
        sum_y = exchange(sy, ry, 1, flip(4))
        x_copies = to_x + to_y + [sum_x, sum_y]
        arrived(3)
        send_shard(flip(6), False, flip(1), 6, ("d0", "d1"))
        for copy, got, start in ((sum_x, rx, 0), (sum_y, ry, edge)):
            copy.wait_recv()
            cols = pl.ds(start, edge)
            g = og[:, cols] + got[0].astype(F32)
            u = ou[:, cols] + got[1].astype(F32)
            hs[:, cols] = (g / (1.0 + jnp.exp(-g)) * u).astype(BF16)
        arrived(6)
    else:
        x_copies = []
        for copy in hid_copies:
            copy.wait_recv()
        for slot in range(n - 1):
            arrived(slot)
        for copy in loads[7:]:
            copy.wait()

        @pl.loop(0, inner // tile)
        def _(c):
            cols = pl.ds(pl.multiple_of(c * tile, tile), tile)
            g = jnp.zeros((rows, tile), F32)
            u = jnp.zeros((rows, tile), F32)
            for i in range(n):
                a = hid[:, :, i * rows_in : (i + 1) * rows_in].reshape(rows, rows_in)
                g = g + mm(a, fg[i, :, cols])
                u = u + mm(a, fu[i, :, cols])
            hs[:, cols] = (g / (1.0 + jnp.exp(-g)) * u).astype(BF16)

    wide = fd.shape[2]

    part2_copies = []
    for side in range(2):

        @pl.loop(side * n // 2, (side + 1) * n // 2)
        def _(i):
            cols = pl.ds(pl.multiple_of(i * wide, wide), wide)
            part2[:, :, cols] = mm(hs[...], fd[i]).astype(BF16).reshape(m, share, wide)

        span = pl.ds(side * middle, middle)
        part2_copies += mlp_copies(
            lambda peer: part2.at[peer, :, span],
            lambda k: part2_in.at[k - 1, :, span],
            part2_s,
            part2_r,
            side * (m - 1),
        )
    total = part2[mj].astype(F32)
    for copy in part2_copies:
        copy.wait_recv()
    for k in range(m - 1):
        total = total + part2_in[k].astype(F32)
    mixed[...] = (res[...] + total).astype(BF16)

    keep.wait()
    for copy in st_copies:
        copy.wait()
    for copy in tok_copies + part_copies + hid_copies + part2_copies + x_copies:
        copy.wait_send()
    for copy in w_copies.values():
        copy.wait_send()


def widen(x, rows_in, out, rows_out, narrow, wide, in_sem, out_sem, row_sem):
    through = pltpu.make_async_copy(rows_in, rows_out, row_sem.at[0])
    through.start()
    count = x.shape[0]
    reads, writes = [], []
    for r in range(count):
        reads.append(pltpu.make_async_copy(x.at[r], narrow.at[r], in_sem.at[r]))
        reads[r].start()
    for r in range(count):
        reads[r].wait()
        wide[r] = narrow[r].astype(F32)
        writes.append(pltpu.make_async_copy(wide.at[r], out.at[r], out_sem.at[r]))
        writes[r].start()
    through.wait()
    for copy in writes:
        copy.wait()


def per_device(
    tokens,
    cached_states,
    prompt_lengths,
    accepted,
    owner_slot,
    w_query,
    w_key,
    w_value,
    w_gate_ret,
    w_out,
    w_gate,
    w_up,
    w_down,
):
    requests, heads, dk, dv = cached_states.shape
    n = lax.axis_size("req")
    m = lax.axis_size("mlp")
    share, width = tokens.shape
    rows = requests * DRAFT
    vmem = pl.BlockSpec(memory_space=pltpu.VMEM)
    smem = pl.BlockSpec(memory_space=pltpu.SMEM)
    hbm = pl.BlockSpec(memory_space=pl.ANY)
    dma = pltpu.SemaphoreType.DMA

    def v(shape, dtype=BF16):
        return pltpu.VMEM(shape, dtype)

    mixed, moved = pl.pallas_call(
        functools.partial(kernel, n, m),
        out_shape=(
            jax.ShapeDtypeStruct((share, width), BF16),
            jax.ShapeDtypeStruct((requests, heads, dk, dv), BF16),
        ),
        in_specs=[smem] * 3 + [hbm] * 10,
        out_specs=(vmem, hbm),
        scratch_shapes=[
            v(w_query.shape),
            v(w_key.shape),
            v(w_value.shape),
            v(w_gate_ret.shape),
            v(w_out.shape),
            v(cached_states.shape, F32),
            v((n,) + w_gate.shape),
            v((n,) + w_up.shape),
            v((n,) + w_down.shape),
            v((m, share, width)),
            v((rows, width)),
            v((rows, heads * dk)),
            v((requests, DRAFT, heads * dk)),
            v((requests, DRAFT, heads * dv)),
            v((rows, heads * dk)),
            v((rows, heads * dv), F32),
            v((rows, heads * dv), F32),
            v((rows, heads * dv)),
            v((m, share, width)),
            v((m - 1, share, width)),
            v((share, width), F32),
            v((m, share, width)),
            v((rows, w_gate.shape[1])),
            v((m, share, width)),
            v((m - 1, share, width)),
            v(cached_states.shape),
            v((m, share, 4 * w_gate.shape[0])),
            v((m, share, 4 * w_gate.shape[0])),
            v((2, rows, w_gate.shape[1] // 2)),
            v((2, rows, w_gate.shape[1] // 2)),
            v((2, rows, w_gate.shape[1] // 2)),
            v((2, rows, w_gate.shape[1] // 2)),
            v((rows, w_gate.shape[1]), F32),
            v((rows, w_gate.shape[1]), F32),
            dma((11,)),
            dma((m - 1,)),
            dma((m - 1,)),
            dma((2 * (m - 1),)),
            dma((2 * (m - 1),)),
            dma((m - 1,)),
            dma((m - 1,)),
            dma((2 * (m - 1),)),
            dma((2 * (m - 1),)),
            dma((n - 1, 4)),
            dma((n - 1, 4)),
            dma((n - 1,)),
            dma((n - 1,)),
            dma((2 + 4 * m,)),
            dma((2 + 4 * m,)),
        ],
        compiler_params=pltpu.CompilerParams(
            collective_id=0, has_side_effects=True, vmem_limit_bytes=60 * 1024 * 1024
        ),
    )(
        prompt_lengths,
        accepted,
        owner_slot,
        tokens,
        cached_states,
        w_query,
        w_key,
        w_value,
        w_gate_ret,
        w_out,
        w_gate,
        w_up,
        w_down,
    )
    mixed, new_states = pl.pallas_call(
        widen,
        out_shape=(
            jax.ShapeDtypeStruct(mixed.shape, BF16),
            jax.ShapeDtypeStruct(moved.shape, F32),
        )[::-1],
        in_specs=[hbm] * 2,
        out_specs=(hbm, hbm),
        scratch_shapes=[
            v(moved.shape),
            v(moved.shape, F32),
            dma((requests,)),
            dma((requests,)),
            dma((1,)),
        ],
        compiler_params=pltpu.CompilerParams(vmem_limit_bytes=32 * 1024 * 1024),
    )(moved, mixed)[::-1]
    return (mixed, new_states)


def solution(mesh):
    return jax.shard_map(
        per_device,
        mesh=mesh,
        in_specs=(
            P(("req", "mlp"), None),
            P("req", "mlp", None, None),
            P("req"),
            P("req"),
            P("req"),
            P(None, "mlp"),
            P(None, "mlp"),
            P(None, "mlp"),
            P(None, "mlp"),
            P("mlp", None),
            P("req", "mlp"),
            P("req", "mlp"),
            P("mlp", "req"),
        ),
        out_specs=(P(("req", "mlp"), None), P("req", "mlp", None, None)),
        check_vma=False,
    )
```

```python
import functools
import math

import jax
import jax.numpy as jnp
from jax import lax
from jax.experimental import pallas as pl
from jax.experimental.pallas import tpu as pltpu
from jax.sharding import PartitionSpec as P

DRAFT = 16


epsilon = 1e-05


def layer_norm(inputs):
    average = jnp.mean(inputs, axis=-1, keepdims=True)
    centred = inputs - average
    variance = jnp.mean(centred * centred, axis=-1, keepdims=True)
    return centred * lax.rsqrt(variance + epsilon)


MESH = pl.DeviceIdType.MESH
F32 = jnp.float32
BF16 = jnp.bfloat16


def mm(a, b):
    return jnp.dot(a, b, preferred_element_type=F32)


def kernel(
    n,
    m,
    prompt,
    accepted,
    slots,
    tokens,
    states,
    w_query,
    w_key,
    w_value,
    w_gate_ret,
    w_out,
    w_gate,
    w_up,
    w_down,
    mixed,
    moved,
    wq,
    wk,
    wv,
    wgr,
    wo,
    st,
    fg,
    fu,
    fd,
    tok,
    normed,
    rq,
    ksc,
    vals,
    rk_h,
    gated,
    outs,
    joined,
    part,
    part_in,
    res,
    hid,
    hs,
    part2,
    part2_in,
    send_buf,
    hx,
    hy,
    sx,
    sy,
    rx,
    ry,
    og,
    ou,
    load_sem,
    tok_s,
    tok_r,
    part_s,
    part_r,
    hid_s,
    hid_r,
    part2_s,
    part2_r,
    w_s,
    w_r,
    st_s,
    st_r,
    x_s,
    x_r,
):
    me = lax.axis_index("req")
    mj = lax.axis_index("mlp")
    share, width = tokens.shape
    requests, heads, dk, dv = states.shape
    rows = m * share
    half = dk // 2
    per_peer = requests // n
    draft = DRAFT

    barrier = pltpu.get_barrier_semaphore()
    for k in range(1, n):
        pl.semaphore_signal(
            barrier, inc=1, device_id={"req": lax.rem(me + k, n)}, device_id_type=MESH
        )
    for k in range(1, m):
        pl.semaphore_signal(
            barrier, inc=1, device_id={"mlp": lax.rem(mj + k, m)}, device_id_type=MESH
        )

    loads = []
    for a, b in (
        (tokens, tok.at[mj]),
        (w_query, wq),
        (w_key, wk),
        (w_value, wv),
        (w_gate_ret, wgr),
        (states, st),
        (w_out, wo),
        (w_gate, fg.at[me]),
        (w_up, fu.at[me]),
        (w_down, fd.at[me]),
    ):
        copy = pltpu.make_async_copy(a, b, load_sem.at[len(loads)])
        copy.start()
        loads.append(copy)

    pl.semaphore_wait(barrier, n + m - 2)

    def mlp_copies(pick, dst, s, r, base=0):
        copies = []
        for k in range(1, m):
            peer = lax.rem(mj + k, m)
            copies.append(
                pltpu.make_async_remote_copy(
                    src_ref=pick(peer),
                    dst_ref=dst(k),
                    send_sem=s.at[base + k - 1],
                    recv_sem=r.at[base + k - 1],
                    device_id={"mlp": peer},
                    device_id_type=MESH,
                )
            )
        for copy in copies:
            copy.start()
        return copies

    tok_copies = mlp_copies(lambda peer: tokens, lambda k: tok.at[mj], tok_s, tok_r)

    cut = w_down.shape[0] // 2
    edge = w_gate.shape[1] // 2
    both = pl.ds(0, w_gate.shape[0])
    cut_of = {
        "g": (w_gate, fg, ()),
        "u": (w_up, fu, ()),
        "ga": (w_gate, fg, (both, pl.ds(0, edge))),
        "gb": (w_gate, fg, (both, pl.ds(edge, edge))),
        "ua": (w_up, fu, (both, pl.ds(0, edge))),
        "ub": (w_up, fu, (both, pl.ds(edge, edge))),
        "d0": (w_down, fd, (pl.ds(0, cut),)),
        "d1": (w_down, fd, (pl.ds(cut, cut),)),
    }

    w_copies = {}

    def send_shard(owner, own, peer, slot, names=("g", "u", "d0", "d1"), at=0):
        for i, name in enumerate(names):
            given, held, where = cut_of[name]
            there = held.at[(owner,) + where]
            copy = pltpu.make_async_remote_copy(
                src_ref=(given.at[where] if where else given) if own else there,
                dst_ref=there,
                send_sem=w_s.at[slot, at + i],
                recv_sem=w_r.at[slot, at + i],
                device_id={"req": peer},
                device_id_type=MESH,
            )
            copy.start()
            w_copies[slot, at + i] = copy

    def arrived(slot):
        for (at, _), copy in w_copies.items():
            if at == slot:
                copy.wait_recv()

    def flip(bits):
        out = me
        for bit in (1, 2, 4):
            if bits & bit:
                out = out + bit - 2 * bit * lax.rem(out // bit, 2)
        return out

    if n == 8:
        side_x = ("gb", "ub", "d0", "d1")
        side_y = ("ga", "ua", "d0", "d1")
        send_shard(me, True, flip(2), 0, side_x)
        send_shard(me, True, flip(4), 1, side_y)
        send_shard(me, True, flip(1), 2)
    else:
        for k in range(1, n):
            send_shard(me, True, lax.rem(me + k, n), k - 1)

    row = lax.broadcasted_iota(jnp.int32, (rows, half), 0)
    draft_pos = lax.rem(row, draft)
    start = jnp.zeros((rows, half), jnp.int32)
    kept = jnp.zeros((rows, half), jnp.int32)
    for r in range(requests):
        start = jnp.where(row >= r * draft, prompt[r], start)
        kept = jnp.where(row >= r * draft, accepted[r], kept)
    lane = lax.broadcasted_iota(jnp.int32, (rows, half), 1).astype(F32)
    angles = (start + draft_pos).astype(F32) * jnp.exp(-math.log(10000.0) * lane / half)
    cos_part, sin_part = jnp.cos(angles), jnp.sin(angles)
    exponent = (kept - 1 - draft_pos).astype(F32)
    to = lax.broadcasted_iota(jnp.int32, (rows, rows), 0)
    source = lax.broadcasted_iota(jnp.int32, (rows, rows), 1)
    causal = (to // draft == source // draft) & (to >= source)
    distance = (to - source).astype(F32)

    def log_gamma(h, shape):
        head = jnp.full(shape, mj * heads + h, jnp.int32).astype(F32)
        return jnp.log(1.0 - jnp.exp2(-5.0 - head))

    fold, mask, carry = [], [], []
    for h in range(heads):
        lg = log_gamma(h, (1, half))
        weight = jnp.where(exponent >= 0, jnp.exp(jnp.maximum(exponent, 0.0) * lg), 0.0)
        fold.append(jnp.concatenate([weight, weight], axis=-1))
        carry.append(jnp.exp((draft_pos.astype(F32) + 1.0) * lg)[:, :1])
        mask.append(
            jnp.where(
                causal, jnp.exp(jnp.maximum(distance, 0.0) * log_gamma(h, (1, rows))), 0.0
            )
        )

    loads[0].wait()
    for copy in tok_copies:
        copy.wait_recv()
    normed[...] = layer_norm(tok[...].astype(F32).reshape(rows, width)).astype(BF16)

    def turned(v):
        front, back = v[:, :half], v[:, half:]
        return jnp.concatenate(
            [front * cos_part - back * sin_part, front * sin_part + back * cos_part], axis=-1
        ).astype(BF16)

    loads[1].wait()
    loads[2].wait()
    for h in range(heads):
        cols = pl.ds(h * dk, dk)
        rq[:, cols] = turned(mm(normed[...], wq[:, cols]))
        rk = turned(mm(normed[...], wk[:, cols]) * (1.0 / math.sqrt(dk)))
        rk_h[:, cols] = rk
        ksc[:, :, cols] = (
            (rk.astype(F32) * fold[h]).astype(BF16).reshape(requests, draft, dk)
        )
    loads[3].wait()
    for h in range(heads):
        cols = pl.ds(h * dv, dv)
        vals[:, :, cols] = mm(normed[...], wv[:, cols]).astype(BF16).reshape(
            requests, draft, dv
        )
    loads[5].wait()

    st_copies = []

    def fresh(p):
        r = 0
        for q in range(requests):
            slot = slots[q]
            place = slot // requests * per_peer + lax.rem(slot, per_peer)
            r = jnp.where(place == p, q, r)
        count = jnp.full((1, dv), accepted[r], jnp.int32).astype(F32)
        for h in range(heads):
            old_scale = jnp.exp(count * log_gamma(h, (1, dv)))
            update = lax.dot_general(
                ksc[r, :, h * dk : (h + 1) * dk],
                vals[r, :, h * dv : (h + 1) * dv],
                (((0,), (0,)), ((), ())),
                preferred_element_type=F32,
            )
            send_buf[p, h] = (old_scale * st[r, h] + update).astype(BF16)

    pl.loop(0, requests)(fresh)
    mine = pl.ds(me * per_peer, per_peer)

    def send_states(peer, slot, keys=pl.ds(0, dk)):
        copy = pltpu.make_async_remote_copy(
            src_ref=send_buf.at[pl.ds(peer * per_peer, per_peer), :, keys],
            dst_ref=moved.at[mine, :, keys],
            send_sem=st_s.at[slot],
            recv_sem=st_r.at[slot],
            device_id={"req": peer},
            device_id_type=MESH,
        )
        copy.start()
        st_copies.append(copy)

    if n == 8:
        for bits in (2, 4, 6, 3, 5, 1):
            send_states(flip(bits), bits - 1)
    else:
        for k in range(1, n):
            send_states(lax.rem(me + k, n), k - 1)
    keep = pltpu.make_async_copy(send_buf.at[mine], moved.at[mine], load_sem.at[10])
    keep.start()

    loads[4].wait()
    for h in range(heads):
        cols = pl.ds(h * dv, dv)
        g = mm(normed[...], wgr[:, cols])
        gated[:, cols] = g / (1.0 + jnp.exp(-g))

    @pl.loop(0, requests)
    def _(r):
        here = pl.ds(pl.multiple_of(r * draft, draft), draft)
        for h in range(heads):
            outs[here, h * dv : (h + 1) * dv] = mm(
                rq[here, h * dk : (h + 1) * dk], st[r, h].astype(BF16)
            )

    for h in range(heads):
        cols = pl.ds(h * dk, dk)
        vcols = pl.ds(h * dv, dv)
        scores = lax.dot_general(
            rq[:, cols], rk_h[:, cols], (((1,), (1,)), ((), ())), preferred_element_type=F32
        )
        weights = (scores * mask[h]).astype(BF16)
        out = mm(weights, vals[:, :, vcols].reshape(rows, dv)) + outs[:, vcols] * carry[h]
        joined[:, vcols] = (layer_norm(out) * gated[:, vcols]).astype(BF16)

    loads[6].wait()
    step = min(512, width // 2)

    middle = width // 2
    part_copies = []
    for side in range(2):

        @pl.loop(0, middle // step)
        def _(c):
            cols = pl.ds(pl.multiple_of(side * middle + c * step, step), step)
            part[:, :, cols] = (
                mm(joined[...], wo[:, cols]).astype(BF16).reshape(m, share, step)
            )

        span = pl.ds(side * middle, middle)
        part_copies += mlp_copies(
            lambda peer: part.at[peer, :, span],
            lambda k: part_in.at[k - 1, :, span],
            part_s,
            part_r,
            side * (m - 1),
        )

    if n == 8:
        arrived(0)
        send_shard(flip(2), False, flip(4), 3, ("d0",))
        arrived(1)
        send_shard(flip(4), False, flip(2), 3, ("d1",), 1)
        send_shard(flip(2), False, flip(1), 4, side_x)
        send_shard(flip(4), False, flip(1), 5, side_y)

    total = part[mj].astype(F32)
    for copy in part_copies:
        copy.wait_recv()
    for k in range(m - 1):
        total = total + part_in[k].astype(F32)
    residual = tok[mj].astype(F32) + total
    res[...] = residual
    hid[mj] = layer_norm(residual).astype(BF16)
    hid_copies = mlp_copies(lambda peer: hid.at[mj], lambda k: hid.at[mj], hid_s, hid_r)

    rows_in = fg.shape[1]
    inner = fg.shape[2]
    tile = min(256, inner // 2)
    if n == 8:
        pair = 2 * rows_in

        def lanes(i):
            return pl.ds(pl.multiple_of(i // 2 * pair, pair), pair)

        def exchange(source, there, slot, peer):
            copy = pltpu.make_async_remote_copy(
                src_ref=source,
                dst_ref=there,
                send_sem=x_s.at[slot],
                recv_sem=x_r.at[slot],
                device_id={"req": peer},
                device_id_type=MESH,
            )
            copy.start()
            return copy

        near, far = pl.ds(0, pair), pl.ds(pair, pair)
        to_x, to_y = [], []
        for k in range(m):
            if k > 0:
                hid_copies[k - 1].wait_recv()
            came = lax.rem(mj + m - k, m)
            at = 2 + 4 * k
            chunk = hid.at[came]
            to_x += [
                exchange(chunk.at[:, lanes(flip(2))], hx.at[came, :, near], at, flip(2)),
                exchange(chunk.at[:, lanes(flip(6))], hx.at[came, :, far], at + 1, flip(2)),
            ]
            to_y += [
                exchange(chunk.at[:, lanes(flip(4))], hy.at[came, :, near], at + 2, flip(4)),
                exchange(chunk.at[:, lanes(flip(6))], hy.at[came, :, far], at + 3, flip(4)),
            ]
        send_states(flip(7), 6, pl.ds(0, half))
        for slot in (2, 4, 5):
            arrived(slot)
        for copy in loads[7:]:
            copy.wait()

        def partial_sums(other, start, mate, theirs):
            @pl.loop(0, edge // tile)
            def _(c):
                cols = pl.ds(pl.multiple_of(start + c * tile, tile), tile)
                g = jnp.zeros((2 * rows, tile), F32)
                u = jnp.zeros((2 * rows, tile), F32)
                for place, base in ((near, me // 2), (far, mate // 2)):
                    a = jnp.concatenate(
                        [
                            hid[:, :, lanes(2 * base)].reshape(rows, pair),
                            other[:, :, place].reshape(rows, pair),
                        ],
                        axis=0,
                    )
                    for odd in range(2):
                        piece = a[:, odd * rows_in : (odd + 1) * rows_in]
                        g = g + mm(piece, fg[2 * base + odd, :, cols])
                        u = u + mm(piece, fu[2 * base + odd, :, cols])
                og[:, cols] = g[:rows]
                ou[:, cols] = u[:rows]
                here = pl.ds(pl.multiple_of(c * tile, tile), tile)
                theirs[0, :, here] = g[rows:].astype(BF16)
                theirs[1, :, here] = u[rows:].astype(BF16)

        for copy in to_x:
            copy.wait_recv()
        partial_sums(hx, 0, flip(4), sx)
        sum_x = exchange(sx, rx, 0, flip(2))
        for copy in to_y:
            copy.wait_recv()
        partial_sums(hy, edge, flip(2), sy)
        sum_y = exchange(sy, ry, 1, flip(4))
        send_states(flip(7), 7, pl.ds(half, half))
        x_copies = to_x + to_y + [sum_x, sum_y]
        arrived(3)
        send_shard(flip(6), False, flip(1), 6, ("d0", "d1"))
        for copy, got, start in ((sum_x, rx, 0), (sum_y, ry, edge)):
            copy.wait_recv()
            cols = pl.ds(start, edge)
            g = og[:, cols] + got[0].astype(F32)
            u = ou[:, cols] + got[1].astype(F32)
            hs[:, cols] = (g / (1.0 + jnp.exp(-g)) * u).astype(BF16)
        arrived(6)
    else:
        x_copies = []
        for copy in hid_copies:
            copy.wait_recv()
        for slot in range(n - 1):
            arrived(slot)
        for copy in loads[7:]:
            copy.wait()

        @pl.loop(0, inner // tile)
        def _(c):
            cols = pl.ds(pl.multiple_of(c * tile, tile), tile)
            g = jnp.zeros((rows, tile), F32)
            u = jnp.zeros((rows, tile), F32)
            for i in range(n):
                a = hid[:, :, i * rows_in : (i + 1) * rows_in].reshape(rows, rows_in)
                g = g + mm(a, fg[i, :, cols])
                u = u + mm(a, fu[i, :, cols])
            hs[:, cols] = (g / (1.0 + jnp.exp(-g)) * u).astype(BF16)

    wide = fd.shape[2]

    part2_copies = []
    for side in range(2):

        @pl.loop(side * n // 2, (side + 1) * n // 2)
        def _(i):
            cols = pl.ds(pl.multiple_of(i * wide, wide), wide)
            part2[:, :, cols] = mm(hs[...], fd[i]).astype(BF16).reshape(m, share, wide)

        span = pl.ds(side * middle, middle)
        part2_copies += mlp_copies(
            lambda peer: part2.at[peer, :, span],
            lambda k: part2_in.at[k - 1, :, span],
            part2_s,
            part2_r,
            side * (m - 1),
        )
    total = part2[mj].astype(F32)
    for copy in part2_copies:
        copy.wait_recv()
    for k in range(m - 1):
        total = total + part2_in[k].astype(F32)
    mixed[...] = (res[...] + total).astype(BF16)

    keep.wait()
    for copy in st_copies:
        copy.wait()
    for copy in tok_copies + part_copies + hid_copies + part2_copies + x_copies:
        copy.wait_send()
    for copy in w_copies.values():
        copy.wait_send()


def widen(x, rows_in, out, rows_out, narrow, wide, in_sem, out_sem, row_sem):
    through = pltpu.make_async_copy(rows_in, rows_out, row_sem.at[0])
    through.start()
    count = x.shape[0]
    reads, writes = [], []
    for r in range(count):
        reads.append(pltpu.make_async_copy(x.at[r], narrow.at[r], in_sem.at[r]))
        reads[r].start()
    for r in range(count):
        reads[r].wait()
        wide[r] = narrow[r].astype(F32)
        writes.append(pltpu.make_async_copy(wide.at[r], out.at[r], out_sem.at[r]))
        writes[r].start()
    through.wait()
    for copy in writes:
        copy.wait()


def per_device(
    tokens,
    cached_states,
    prompt_lengths,
    accepted,
    owner_slot,
    w_query,
    w_key,
    w_value,
    w_gate_ret,
    w_out,
    w_gate,
    w_up,
    w_down,
):
    requests, heads, dk, dv = cached_states.shape
    n = lax.axis_size("req")
    m = lax.axis_size("mlp")
    share, width = tokens.shape
    rows = requests * DRAFT
    vmem = pl.BlockSpec(memory_space=pltpu.VMEM)
    smem = pl.BlockSpec(memory_space=pltpu.SMEM)
    hbm = pl.BlockSpec(memory_space=pl.ANY)
    dma = pltpu.SemaphoreType.DMA

    def v(shape, dtype=BF16):
        return pltpu.VMEM(shape, dtype)

    mixed, moved = pl.pallas_call(
        functools.partial(kernel, n, m),
        out_shape=(
            jax.ShapeDtypeStruct((share, width), BF16),
            jax.ShapeDtypeStruct((requests, heads, dk, dv), BF16),
        ),
        in_specs=[smem] * 3 + [hbm] * 10,
        out_specs=(vmem, hbm),
        scratch_shapes=[
            v(w_query.shape),
            v(w_key.shape),
            v(w_value.shape),
            v(w_gate_ret.shape),
            v(w_out.shape),
            v(cached_states.shape, F32),
            v((n,) + w_gate.shape),
            v((n,) + w_up.shape),
            v((n,) + w_down.shape),
            v((m, share, width)),
            v((rows, width)),
            v((rows, heads * dk)),
            v((requests, DRAFT, heads * dk)),
            v((requests, DRAFT, heads * dv)),
            v((rows, heads * dk)),
            v((rows, heads * dv), F32),
            v((rows, heads * dv), F32),
            v((rows, heads * dv)),
            v((m, share, width)),
            v((m - 1, share, width)),
            v((share, width), F32),
            v((m, share, width)),
            v((rows, w_gate.shape[1])),
            v((m, share, width)),
            v((m - 1, share, width)),
            v(cached_states.shape),
            v((m, share, 4 * w_gate.shape[0])),
            v((m, share, 4 * w_gate.shape[0])),
            v((2, rows, w_gate.shape[1] // 2)),
            v((2, rows, w_gate.shape[1] // 2)),
            v((2, rows, w_gate.shape[1] // 2)),
            v((2, rows, w_gate.shape[1] // 2)),
            v((rows, w_gate.shape[1]), F32),
            v((rows, w_gate.shape[1]), F32),
            dma((11,)),
            dma((m - 1,)),
            dma((m - 1,)),
            dma((2 * (m - 1),)),
            dma((2 * (m - 1),)),
            dma((m - 1,)),
            dma((m - 1,)),
            dma((2 * (m - 1),)),
            dma((2 * (m - 1),)),
            dma((n - 1, 4)),
            dma((n - 1, 4)),
            dma((n,)),
            dma((n,)),
            dma((2 + 4 * m,)),
            dma((2 + 4 * m,)),
        ],
        compiler_params=pltpu.CompilerParams(
            collective_id=0, has_side_effects=True, vmem_limit_bytes=60 * 1024 * 1024
        ),
    )(
        prompt_lengths,
        accepted,
        owner_slot,
        tokens,
        cached_states,
        w_query,
        w_key,
        w_value,
        w_gate_ret,
        w_out,
        w_gate,
        w_up,
        w_down,
    )
    mixed, new_states = pl.pallas_call(
        widen,
        out_shape=(
            jax.ShapeDtypeStruct(mixed.shape, BF16),
            jax.ShapeDtypeStruct(moved.shape, F32),
        )[::-1],
        in_specs=[hbm] * 2,
        out_specs=(hbm, hbm),
        scratch_shapes=[
            v(moved.shape),
            v(moved.shape, F32),
            dma((requests,)),
            dma((requests,)),
            dma((1,)),
        ],
        compiler_params=pltpu.CompilerParams(vmem_limit_bytes=60 * 1024 * 1024),
    )(moved, mixed)[::-1]
    return (mixed, new_states)


def solution(mesh):
    return jax.shard_map(
        per_device,
        mesh=mesh,
        in_specs=(
            P(("req", "mlp"), None),
            P("req", "mlp", None, None),
            P("req"),
            P("req"),
            P("req"),
            P(None, "mlp"),
            P(None, "mlp"),
            P(None, "mlp"),
            P(None, "mlp"),
            P("mlp", None),
            P("req", "mlp"),
            P("req", "mlp"),
            P("mlp", "req"),
        ),
        out_specs=(P(("req", "mlp"), None), P("req", "mlp", None, None)),
        check_vma=False,
    )
```
